512 devices in a mesh: rep: 4 (over y), dev: 128 (over z, x, core).
Axes of the slice: x: 4, y: 4, z: 16, core: 2. Of those that a mesh axis runs over, the one named last changes fastest.
Arguments:
- params: float32 [59, 65536], P(None, 'dev'), may hold values from -12 to 24, as said below
- adam_m: float32 [59, 65536], P(None, 'dev'), may hold values from -0.6 to 0.6
- adam_v: float32 [59, 65536], P(None, 'dev'), may hold values from 0.001 to 0.1
- target: float32 [4, 128, 2, 3, 256], P('rep', 'dev'), may hold values from 0 to 1
- tile_ids: int32 [4, 128, 2], P('rep', 'dev'), may hold values from 0 to 1023, as said below
- send_blocks: int32 [4, 128, 128, 1], P('rep', 'dev'), may hold values from -1 to 7, as said below
- tile_lists: int32 [4, 128, 2, 8], P('rep', 'dev'), may hold values from -1 to 127, as said below
Outputs:
- new_params: float32 [59, 65536], P(None, 'dev')
- new_m: float32 [59, 65536], P(None, 'dev')
- new_v: float32 [59, 65536], P(None, 'dev')
- grad: float32 [59, 65536], P(None, 'dev')
The draws below stay inside these ranges and needn't reach their ends.
Inputs may be any that keep to these rules, and one draw needn't show every extreme that they name: `tile_ids`: every tile of the 64 x 8 region of each view is assigned to exactly one device. `send_blocks`: A value is view * 4 + block of the owner, or -1 where the owner provides nothing in that slot; the view of every live value equals the view of that renderer's tiles; the live values of one owner for one renderer are distinct blocks. `tile_lists`: A list is either all -1 or holds 8 live entries, front to back; every live entry names a slot whose send_blocks entry for this renderer is live, and the live entries of one renderer are distinct. `params`: row 2 lies in [18, 22], row 10 is at most 1, the quaternion rows have norm at least 0.5.
All inputs are finite; a program needn't handle non-finite values.
Results may differ from the reference program's by a relative error of at most 0.0003.
Values sent between devices are 32-bit elements; how exact they have to be, the bound alone decides.
No kernel may reach another device: no remote copies, remote signals or barrier semaphores. Data moves between devices by JAX's collectives and lax.ppermute only.
A program may use at most 64 MiB of HBM per device.

```python
import math
import jax
import jax.numpy as jnp
from jax import lax

BLOCK = 128
PARAMS = 59
FEATS = 9
VIEWS = 2
TILE = 256
LIST = 8
TILES_X = 64
ADAM_STEP = 1000
BLK_DEV = 4
NB = 512
GAUSS = 65536
TILES_Y = 8
TILES_DEV = 2
PAIR_BLOCKS = 1
N_REP = 4
N_DEV = 128


def scene_layout(key):
    renderers = N_REP * N_DEV
    cells = N_DEV // LIST
    view_renderers = renderers // VIEWS
    regions_x = TILES_X // LIST
    owner_of = jax.random.permutation(jax.random.fold_in(key, 11), N_DEV).astype(jnp.int32)
    order = jax.random.permutation(jax.random.fold_in(key, 13), renderers).astype(jnp.int32)
    which_view = order // view_renderers
    index_in_view = order % view_renderers
    region_scores = jax.random.randint(jax.random.fold_in(key, 14), (VIEWS, cells, BLK_DEV), 0, 65536, jnp.int32) * BLK_DEV + jnp.arange(BLK_DEV, dtype=jnp.int32)
    region_perm = jnp.argsort(region_scores, axis=-1, stable=True).astype(jnp.int32)
    place_scores = jax.random.randint(jax.random.fold_in(key, 15), (VIEWS, cells, LIST), 0, 65536, jnp.int32) * LIST + jnp.arange(LIST, dtype=jnp.int32)
    place_perm = jnp.argsort(place_scores, axis=-1, stable=True).astype(jnp.int32)
    spot = jnp.arange(TILES_DEV, dtype=jnp.int32)
    flat = index_in_view[:, None] * TILES_DEV + spot[None, :]
    cell = flat % cells
    rank = flat // cells
    view_col = which_view[:, None] + jnp.zeros_like(cell)
    in_cell = region_perm[view_col, cell, rank % BLK_DEV]
    in_region = place_perm[view_col, cell, rank // BLK_DEV]
    region = cell * BLK_DEV + in_cell
    home_x = region % regions_x * LIST + in_region
    home_y = region // regions_x
    tile_x = (home_x - view_col) % TILES_X
    live = home_x >= view_col
    tile_nums = view_col * (TILES_X * TILES_Y) + home_y * TILES_X + tile_x
    layers = jnp.arange(LIST, dtype=jnp.int32)
    owner = owner_of[layers[None, None, :] * cells + cell[:, :, None]]
    which_slot = spot // cells
    slot = owner * PAIR_BLOCKS + which_slot[None, :, None]
    lists = jnp.where(live[:, :, None], slot, -1)
    width = N_DEV * PAIR_BLOCKS
    code = jnp.broadcast_to((view_col * BLK_DEV + in_cell)[:, :, None], slot.shape)
    columns = jnp.where(live[:, :, None], slot, width)
    rows = jnp.broadcast_to(jnp.arange(renderers, dtype=jnp.int32)[:, None, None], slot.shape)
    sends = jnp.full((renderers, width), -1, jnp.int32).at[rows, columns].set(code, mode='drop')
    return (tile_nums.astype(jnp.int32), sends.reshape(renderers, N_DEV, PAIR_BLOCKS), lists.astype(jnp.int32), owner_of)


def draw_tile_ids(key, part):
    layout = scene_layout(key)
    return layout[0].reshape(N_REP, N_DEV, TILES_DEV).astype(jnp.int32)


def draw_send_blocks(key, part):
    layout = scene_layout(key)
    return layout[1].reshape(N_REP, N_DEV, N_DEV, PAIR_BLOCKS).transpose(0, 2, 1, 3).astype(jnp.int32)


def draw_tile_lists(key, part):
    layout = scene_layout(key)
    return layout[2].reshape(N_REP, N_DEV, TILES_DEV, LIST).astype(jnp.int32)


def draw_params(key, part):
    layout = scene_layout(key)
    owner_of = layout[3]
    key = jax.random.fold_in(key, 21)
    streams = jax.random.split(key, 7)
    inset = 3.0
    low_sigma = 1.0
    high_sigma = 3.0
    top_logit = 0.0
    cells = N_DEV // LIST
    regions_x = TILES_X // LIST
    place = jnp.zeros((N_DEV,), jnp.int32).at[owner_of].set(jnp.arange(N_DEV, dtype=jnp.int32))
    block = jnp.arange(GAUSS, dtype=jnp.int32) // BLOCK
    owner = block // BLK_DEV
    local = block % BLK_DEV
    layer_cell = place[owner]
    layer = layer_cell // cells
    cell = layer_cell % cells
    region = cell * BLK_DEV + local
    region_x = (region % regions_x).astype(jnp.float32)
    region_y = (region // regions_x).astype(jnp.float32)
    spot = jax.random.uniform(streams[0], (2, GAUSS), jnp.float32, 0.0, 1.0)
    screen_x = 16.0 * LIST * region_x + inset + spot[0] * (16.0 * LIST - 2.0 * inset)
    screen_y = 16.0 * region_y + inset + spot[1] * (16.0 - 2.0 * inset)
    within = jax.random.uniform(streams[1], (GAUSS,), jnp.float32, 0.1, 0.9)
    depth = 20.0 * (0.95 + 0.1 * (layer.astype(jnp.float32) + within) / LIST)
    world_x = (screen_x - 8.0 * TILES_X) * depth / 1100.0
    world_y = (screen_y - 8.0 * TILES_Y) * depth / 1100.0
    sigma = jnp.exp(jax.random.uniform(streams[2], (3, GAUSS), jnp.float32, math.log(low_sigma), math.log(high_sigma)))
    log_scale = jnp.log(sigma * depth[None, :] / 1100.0)
    quat_w = jax.random.uniform(streams[3], (1, GAUSS), jnp.float32, 0.5, 1.5)
    quat_rest = jax.random.uniform(streams[4], (3, GAUSS), jnp.float32, -1.0, 1.0)
    logit = jax.random.uniform(streams[5], (1, GAUSS), jnp.float32, -5.0, top_logit)
    weights = jnp.concatenate([jnp.ones((1, 1, 1), jnp.float32), jnp.full((15, 1, 1), 0.3, jnp.float32)], axis=0)
    coeffs = jnp.clip(jax.random.normal(streams[6], (16, 3, GAUSS), jnp.float32), -4.0, 4.0) * weights
    rows = jnp.concatenate([world_x[None], world_y[None], depth[None], log_scale, quat_w, quat_rest, logit, coeffs.reshape(48, GAUSS)], axis=0)
    return rows.astype(jnp.float32)


def levels(rng, extent, cuts, low, high):
    gain, own = 1.0, jax.random.fold_in(rng, 6)
    for dim, parts in cuts:
        heights = jnp.exp(jax.random.uniform(jax.random.fold_in(own, dim), (parts,), jnp.float32, low / len(cuts), high / len(cuts)))
        gain = gain * jnp.repeat(heights, extent[dim] // parts).reshape([-1 if axis == dim else 1 for axis in range(len(extent))])
    return gain


def normal_values(own_key, dims, deviation, most, cuts=(), held_as=jnp.bfloat16):
    entries = jax.random.normal(own_key, dims, jnp.float32) * deviation
    if len(cuts) > 0:
        entries = levels(own_key, dims, cuts, -0.22, 0.18) * entries
    return jnp.clip(entries, min=-most, max=most).astype(held_as)


def setup_inputs(seed: int = 0) -> dict:
    streams_of = jax.random.split(jax.random.key(seed), 8)
    params = draw_params(jax.random.fold_in(streams_of[7], 71), 0)
    adam_m = normal_values(streams_of[1], (PARAMS, GAUSS), 0.1, 0.6, ((1, 128),), jnp.float32)
    adam_v = jnp.clip(jnp.exp(math.log(0.1) - 4.6051702 * jax.random.uniform(streams_of[2], (PARAMS, GAUSS), jnp.float32) ** levels(streams_of[2], (PARAMS, GAUSS), ((1, 128),), -0.2, 0.2)), 0.001, 0.1)
    target = jnp.clip(1.0 * jax.random.uniform(streams_of[3], (N_REP, N_DEV, TILES_DEV, 3, TILE), jnp.float32) ** levels(streams_of[3], (N_REP, N_DEV, TILES_DEV, 3, TILE), ((0, 4), (1, 128)), -0.2, 0.2), 0.0, 1.0)
    tile_ids = draw_tile_ids(jax.random.fold_in(streams_of[7], 71), 0)
    send_blocks = draw_send_blocks(jax.random.fold_in(streams_of[7], 71), 0)
    tile_lists = draw_tile_lists(jax.random.fold_in(streams_of[7], 71), 0)
    return dict(params=params, adam_m=adam_m, adam_v=adam_v, target=target, tile_ids=tile_ids, send_blocks=send_blocks, tile_lists=tile_lists)


FOCAL = 1100.0
DEPTH_ZERO = 20.0
BASELINE = 16.0 * DEPTH_ZERO / FOCAL
BLUR = 0.3
SMOOTHING = 0.0001
BETA_ONE = 0.9
BETA_TWO = 0.999
ADAM_EPS = 1e-15
SH_ZERO = 0.28209479177387814
SH_ONE = 0.4886025119029199
SH_TWO = [1.0925484305920792, -1.0925484305920792, 0.31539156525252005, -1.0925484305920792, 0.5462742152960396]
SH_THREE = [-0.5900435899266435, 2.890611442640554, -0.4570457994644658, 0.3731763325901154, -0.4570457994644658, 1.445305721320277, -0.5900435899266435]
RATE_LIST = [0.00016] * 3 + [0.005] * 3 + [0.001] * 4 + [0.05] + [0.0025] * 3 + [0.000125] * 45

def sh_basis(unit_x, unit_y, unit_z):
    square_x = unit_x * unit_x
    square_y = unit_y * unit_y
    square_z = unit_z * unit_z
    return [SH_ZERO + 0.0 * unit_x, -SH_ONE * unit_y, SH_ONE * unit_z, -SH_ONE * unit_x, SH_TWO[0] * unit_x * unit_y, SH_TWO[1] * unit_y * unit_z, SH_TWO[2] * (2.0 * square_z - square_x - square_y), SH_TWO[3] * unit_x * unit_z, SH_TWO[4] * (square_x - square_y), SH_THREE[0] * unit_y * (3.0 * square_x - square_y), SH_THREE[1] * unit_x * unit_y * unit_z, SH_THREE[2] * unit_y * (4.0 * square_z - square_x - square_y), SH_THREE[3] * unit_z * (2.0 * square_z - 3.0 * square_x - 3.0 * square_y), SH_THREE[4] * unit_x * (4.0 * square_z - square_x - square_y), SH_THREE[5] * unit_z * (square_x - square_y), SH_THREE[6] * unit_x * (square_x - 3.0 * square_y)]

def project(raw_rows, baseline_shift, center_x, center_y):
    offset_x = raw_rows[0] - baseline_shift
    offset_y = raw_rows[1]
    depth = raw_rows[2]
    inverse = 1.0 / depth
    focal_depth = FOCAL * inverse
    screen_x = focal_depth * offset_x + center_x
    screen_y = focal_depth * offset_y + center_y
    scales = jnp.exp(raw_rows[3:6])
    quaternion = raw_rows[6:10]
    quaternion = quaternion / jnp.sqrt(lax.optimization_barrier(jnp.sum(quaternion * quaternion, axis=0)))
    quat_w, quat_x, quat_y, quat_z = (quaternion[0], quaternion[1], quaternion[2], quaternion[3])
    rotation = [[1.0 - 2.0 * (quat_y * quat_y + quat_z * quat_z), 2.0 * (quat_x * quat_y - quat_w * quat_z), 2.0 * (quat_x * quat_z + quat_w * quat_y)], [2.0 * (quat_x * quat_y + quat_w * quat_z), 1.0 - 2.0 * (quat_x * quat_x + quat_z * quat_z), 2.0 * (quat_y * quat_z - quat_w * quat_x)], [2.0 * (quat_x * quat_z - quat_w * quat_y), 2.0 * (quat_y * quat_z + quat_w * quat_x), 1.0 - 2.0 * (quat_x * quat_x + quat_y * quat_y)]]
    slope_x = focal_depth * offset_x * inverse
    slope_y = focal_depth * offset_y * inverse
    first_row = [(focal_depth * rotation[0][index] - slope_x * rotation[2][index]) * scales[index] for index in range(3)]
    second_row = [(focal_depth * rotation[1][index] - slope_y * rotation[2][index]) * scales[index] for index in range(3)]
    sigma_xx = first_row[0] * first_row[0] + first_row[1] * first_row[1] + first_row[2] * first_row[2] + BLUR
    sigma_xy = first_row[0] * second_row[0] + first_row[1] * second_row[1] + first_row[2] * second_row[2]
    sigma_yy = second_row[0] * second_row[0] + second_row[1] * second_row[1] + second_row[2] * second_row[2] + BLUR
    determinant = sigma_xx * sigma_yy - sigma_xy * sigma_xy
    opacity = jax.nn.sigmoid(raw_rows[10])
    distance = jnp.sqrt(offset_x * offset_x + offset_y * offset_y + depth * depth)
    basis = jnp.stack(sh_basis(offset_x / distance, offset_y / distance, depth / distance))
    coeffs = raw_rows[11:].reshape(16, 3, raw_rows.shape[1])
    color = jnp.maximum(lax.optimization_barrier(jnp.sum(basis[:, None, :] * coeffs, axis=0)) + 0.5, 0.0)
    screen = jnp.stack([screen_x, screen_y, sigma_yy / determinant, -sigma_xy / determinant, sigma_xx / determinant, opacity])
    return jnp.concatenate([screen, color], axis=0)

def render_loss(features, gaussian_mask, anchor_x, anchor_y, goal_tile, prefix_fn):
    pixels = jnp.arange(goal_tile.shape[1], dtype=jnp.int32)
    pixel_x = anchor_x + (pixels % 16).astype(jnp.float32) + 0.5
    pixel_y = anchor_y + (pixels // 16).astype(jnp.float32) + 0.5
    delta_x = pixel_x[:, None] - features[0][None, :]
    delta_y = pixel_y[:, None] - features[1][None, :]
    power = -0.5 * (features[2] * delta_x * delta_x + features[4] * delta_y * delta_y) - features[3] * delta_x * delta_y
    alpha = features[5] * jnp.exp(power) * gaussian_mask
    survive = jnp.log(1.0 - alpha)
    weight = alpha * jnp.exp(prefix_fn(survive))
    color = jnp.einsum('ck,pk->cp', features[6:9], weight, precision=lax.Precision.HIGHEST)
    error = color - goal_tile
    return jnp.sum(jnp.sqrt(error * error + SMOOTHING)) / 3.0

def exclusive_sum(survive):
    return jnp.cumsum(survive, axis=1) - survive

def adam_update(params, adam_m, adam_v, grad):
    new_m = BETA_ONE * adam_m + (1.0 - BETA_ONE) * grad
    new_v = BETA_TWO * adam_v + (1.0 - BETA_TWO) * grad * grad
    m_hat = new_m / (1.0 - BETA_ONE ** ADAM_STEP)
    v_hat = new_v / (1.0 - BETA_TWO ** ADAM_STEP)
    rates = jnp.array(RATE_LIST, jnp.float32)[:, None]
    return (params - rates * m_hat / (jnp.sqrt(v_hat) + ADAM_EPS), new_m, new_v)

def reference(params, adam_m, adam_v, target, tile_ids, send_blocks, tile_lists):
    center_x = 8.0 * TILES_X
    center_y = 8.0 * TILES_Y

    def all_views(values):
        return jnp.stack([project(values, view_index * BASELINE, center_x, center_y) for view_index in range(VIEWS)])
    features, pull = jax.vjp(all_views, params)
    table = features.reshape(VIEWS, FEATS, NB, BLOCK).transpose(0, 2, 1, 3)
    renderers = N_REP * N_DEV
    renderer = jnp.arange(renderers, dtype=jnp.int32)
    rep_of = renderer // N_DEV
    dev_of = renderer % N_DEV
    tile_nums = tile_ids.reshape(renderers, TILES_DEV)
    lists = tile_lists.reshape(renderers, TILES_DEV, LIST)
    goals = target.reshape(renderers, TILES_DEV, 3, TILE)
    per_view = TILES_X * TILES_Y
    views = tile_nums // per_view
    within = tile_nums % per_view
    anchor_x = (within % TILES_X * 16).astype(jnp.float32)
    anchor_y = (within // TILES_X * 16).astype(jnp.float32)
    masks = (lists >= 0).astype(jnp.float32)
    slots = jnp.maximum(lists, 0).astype(jnp.int32)
    owners = (slots // PAIR_BLOCKS).astype(jnp.int32)
    pair_slot = (slots % PAIR_BLOCKS).astype(jnp.int32)
    codes = send_blocks[rep_of[:, None, None], owners, dev_of[:, None, None], pair_slot]
    blocks = (owners * BLK_DEV + codes % BLK_DEV).astype(jnp.int32)

    def tile_cot(view_num, block_ids, block_mask, corner_x, corner_y, goal_tile):

        def loss_of(chosen):
            flat = chosen.transpose(1, 0, 2).reshape(FEATS, LIST * BLOCK)
            return render_loss(flat, jnp.repeat(block_mask, BLOCK), corner_x, corner_y, goal_tile, exclusive_sum)
        chosen = table[view_num, block_ids]
        _, back = jax.vjp(loss_of, chosen)
        return back(jnp.ones((), jnp.float32))[0]

    def step(total, item):
        view_num, block_ids, block_mask, corner_x, corner_y, goal_tile = item
        grads = jax.vmap(tile_cot)(view_num, block_ids, block_mask, corner_x, corner_y, goal_tile)
        total = total.at[view_num[:, None], block_ids].add(grads)
        return (total, None)
    start = jnp.zeros((VIEWS, NB, FEATS, BLOCK), jnp.float32)
    cotangent, _ = lax.scan(step, start, (views, blocks, masks, anchor_x, anchor_y, goals))
    grad = pull(cotangent.transpose(0, 2, 1, 3).reshape(VIEWS, FEATS, GAUSS))[0]
    new_params, new_m, new_v = adam_update(params, adam_m, adam_v, grad)
    return (new_params, new_m, new_v, grad)
```

```python
import jax
import jax.numpy as jnp
from jax import lax
from jax.experimental import pallas as pl
from jax.experimental.pallas import tpu as pltpu
from jax.sharding import PartitionSpec as P

BLOCK = 128
PARAMS = 59
FEATS = 9
SLOT = FEATS * BLOCK
TILE = 256
SIDE = 16
LIST = 8
TILES_X = 64
ADAM_STEP = 1000

FOCAL = 1100.0
DEPTH_ZERO = 20.0
BASELINE = 16.0 * DEPTH_ZERO / FOCAL
BLUR = 0.3
SMOOTHING = 0.0001
BETA_ONE = 0.9
BETA_TWO = 0.999
ADAM_EPS = 1e-15
SH_ZERO = 0.28209479177387814
SH_ONE = 0.4886025119029199
SH_TWO = [
    1.0925484305920792,
    -1.0925484305920792,
    0.31539156525252005,
    -1.0925484305920792,
    0.5462742152960396,
]
SH_THREE = [
    -0.5900435899266435,
    2.890611442640554,
    -0.4570457994644658,
    0.3731763325901154,
    -0.4570457994644658,
    1.445305721320277,
    -0.5900435899266435,
]
RATES = [(0, 0.00016), (3, 0.005), (6, 0.001), (10, 0.05), (11, 0.0025), (14, 0.000125)]

VMEM_LIMIT = 40 * 1024 * 1024
SMEM = pltpu.MemorySpace.SMEM
VMEM = pltpu.MemorySpace.VMEM


def sh_basis(unit_x, unit_y, unit_z):
    square_x = unit_x * unit_x
    square_y = unit_y * unit_y
    square_z = unit_z * unit_z
    return [
        SH_ZERO + 0.0 * unit_x,
        -SH_ONE * unit_y,
        SH_ONE * unit_z,
        -SH_ONE * unit_x,
        SH_TWO[0] * unit_x * unit_y,
        SH_TWO[1] * unit_y * unit_z,
        SH_TWO[2] * (2.0 * square_z - square_x - square_y),
        SH_TWO[3] * unit_x * unit_z,
        SH_TWO[4] * (square_x - square_y),
        SH_THREE[0] * unit_y * (3.0 * square_x - square_y),
        SH_THREE[1] * unit_x * unit_y * unit_z,
        SH_THREE[2] * unit_y * (4.0 * square_z - square_x - square_y),
        SH_THREE[3] * unit_z * (2.0 * square_z - 3.0 * square_x - 3.0 * square_y),
        SH_THREE[4] * unit_x * (4.0 * square_z - square_x - square_y),
        SH_THREE[5] * unit_z * (square_x - square_y),
        SH_THREE[6] * unit_x * (square_x - 3.0 * square_y),
    ]


def project(rows, shift, center_x, center_y):
    offset_x = rows[0] - shift
    offset_y = rows[1]
    depth = rows[2]
    inverse = 1.0 / depth
    focal_depth = FOCAL * inverse
    screen_x = focal_depth * offset_x + center_x
    screen_y = focal_depth * offset_y + center_y
    scales = [jnp.exp(rows[3 + index]) for index in range(3)]
    norm = jnp.sqrt(
        rows[6] * rows[6] + rows[7] * rows[7] + rows[8] * rows[8] + rows[9] * rows[9]
    )
    quat_w, quat_x, quat_y, quat_z = [rows[6 + index] / norm for index in range(4)]
    rotation = [
        [
            1.0 - 2.0 * (quat_y * quat_y + quat_z * quat_z),
            2.0 * (quat_x * quat_y - quat_w * quat_z),
            2.0 * (quat_x * quat_z + quat_w * quat_y),
        ],
        [
            2.0 * (quat_x * quat_y + quat_w * quat_z),
            1.0 - 2.0 * (quat_x * quat_x + quat_z * quat_z),
            2.0 * (quat_y * quat_z - quat_w * quat_x),
        ],
        [
            2.0 * (quat_x * quat_z - quat_w * quat_y),
            2.0 * (quat_y * quat_z + quat_w * quat_x),
            1.0 - 2.0 * (quat_x * quat_x + quat_y * quat_y),
        ],
    ]
    slope_x = focal_depth * offset_x * inverse
    slope_y = focal_depth * offset_y * inverse
    first_row = [
        (focal_depth * rotation[0][index] - slope_x * rotation[2][index]) * scales[index]
        for index in range(3)
    ]
    second_row = [
        (focal_depth * rotation[1][index] - slope_y * rotation[2][index]) * scales[index]
        for index in range(3)
    ]
    sigma_xx = (
        first_row[0] * first_row[0]
        + first_row[1] * first_row[1]
        + first_row[2] * first_row[2]
        + BLUR
    )
    sigma_xy = (
        first_row[0] * second_row[0] + first_row[1] * second_row[1] + first_row[2] * second_row[2]
    )
    sigma_yy = (
        second_row[0] * second_row[0]
        + second_row[1] * second_row[1]
        + second_row[2] * second_row[2]
        + BLUR
    )
    determinant = sigma_xx * sigma_yy - sigma_xy * sigma_xy
    distance = jnp.sqrt(offset_x * offset_x + offset_y * offset_y + depth * depth)
    basis = sh_basis(offset_x / distance, offset_y / distance, depth / distance)
    colors = []
    for channel in range(3):
        total = basis[0] * rows[11 + channel]
        for index in range(1, 16):
            total = total + basis[index] * rows[11 + 3 * index + channel]
        colors.append(jnp.maximum(total + 0.5, 0.0))
    return [
        screen_x,
        screen_y,
        sigma_yy / determinant,
        -sigma_xy / determinant,
        sigma_xx / determinant,
        colors[0],
        colors[1],
        colors[2],
    ]


def code_rows(params_ref, blocks_here):
    rows = []
    for row in range(PARAMS):
        parts = [
            params_ref[row : row + 1, block * BLOCK : (block + 1) * BLOCK]
            for block in range(blocks_here)
        ]
        rows.append(jnp.concatenate(parts + parts, axis=0))
    return rows


def code_shift(blocks_here):
    code = lax.broadcasted_iota(jnp.int32, (2 * blocks_here, BLOCK), 0)
    return jnp.where(code >= blocks_here, BASELINE, 0.0).astype(jnp.float32)


def halves(values, pieces):
    out = []
    rest = values
    for index in range(pieces):
        part = rest.astype(jnp.bfloat16)
        out.append(part)
        if index < pieces - 1:
            rest = rest - part.astype(jnp.float32)
    return out


def project_kernel(blocks_here, center_x, center_y, codes_ref, params_ref, out_ref, table_ref):
    rows = code_rows(params_ref, blocks_here)
    shown = project(rows, code_shift(blocks_here), center_x, center_y)
    shown = shown[:5] + [jax.nn.sigmoid(rows[10])] + shown[5:]
    for code in range(2 * blocks_here):
        for feat in range(FEATS):
            table_ref[code, :, feat * BLOCK : (feat + 1) * BLOCK] = shown[feat][code : code + 1]

    def fill(target, carry):
        code = jnp.maximum(codes_ref[target], 0)
        out_ref[target] = table_ref[code]
        return carry

    lax.fori_loop(0, out_ref.shape[0], fill, 0, unroll=8)


def render_kernel(
    tiles_y,
    ids_ref,
    lists_ref,
    slots_ref,
    goal_ref,
    out_ref,
    alpha_ref,
    weight_ref,
    pieces_ref,
    carry_ref,
    color_ref,
    slope_ref,
):
    tiles = ids_ref.shape[0]
    per_view = TILES_X * tiles_y
    f32 = jnp.float32
    lane = lax.broadcasted_iota(jnp.int32, (2 * BLOCK, 2 * BLOCK), 1)
    depth = lax.broadcasted_iota(jnp.int32, (2 * BLOCK, 2 * BLOCK), 0) % BLOCK
    earlier = jnp.where((lane >= BLOCK) | (depth < lane), 1.0, 0.0).astype(jnp.bfloat16)
    later = jnp.where((lane >= BLOCK) | (depth > lane), 1.0, 0.0).astype(jnp.bfloat16)
    ones = jnp.ones((2 * BLOCK, BLOCK), jnp.bfloat16)
    column = lax.broadcasted_iota(jnp.int32, (SIDE, BLOCK), 0).astype(f32) - (SIDE / 2 - 0.5)

    out_ref[...] = jnp.zeros_like(out_ref)
    carry_ref[...] = jnp.zeros_like(carry_ref)
    color_ref[...] = jnp.zeros_like(color_ref)

    def feature(slot, index):
        return slots_ref[slot, :, index * BLOCK : (index + 1) * BLOCK]

    def center(tile):
        within = lax.rem(ids_ref[tile], per_view)
        middle_x = (lax.rem(within, TILES_X) * SIDE + SIDE // 2).astype(f32)
        middle_y = (lax.div(within, TILES_X) * SIDE + SIDE // 2).astype(f32)
        return middle_x, middle_y

    def row_of(index):
        return slice(index * SIDE, (index + 1) * SIDE)

    def forward(layer, carry):
        for tile in range(tiles):
            entry = lists_ref[tile * LIST + layer]
            slot = jnp.maximum(entry, 0)
            live = jnp.where(entry >= 0, 1.0, 0.0).astype(f32)
            middle_x, middle_y = center(tile)
            delta_x = column - (feature(slot, 0) - middle_x)
            place_y = feature(slot, 1) - middle_y
            half_x = (-0.5 * feature(slot, 2)) * delta_x * delta_x
            cross = -feature(slot, 3) * delta_x
            half_y = jnp.broadcast_to(-0.5 * feature(slot, 4), (SIDE, BLOCK))
            opacity = jnp.broadcast_to(feature(slot, 5) * live, (SIDE, BLOCK))
            place_y = jnp.broadcast_to(place_y, (SIDE, BLOCK))
            for row in range(SIDE):
                delta_y = (row - (SIDE / 2 - 0.5)) - place_y
                power = half_x + delta_y * (cross + half_y * delta_y)
                alpha = opacity * jnp.exp(power)
                alpha_ref[tile, layer, row_of(row)] = alpha
                high, low = halves(jnp.log(1.0 - alpha), 2)
                start = tile * TILE + row * SIDE
                pieces_ref[start : start + SIDE, :BLOCK] = high
                pieces_ref[start : start + SIDE, BLOCK:] = low
        sums = jnp.dot(pieces_ref[...], earlier, preferred_element_type=f32)
        for tile in range(tiles):
            slot = jnp.maximum(lists_ref[tile * LIST + layer], 0)
            shades = [
                jnp.broadcast_to(feature(slot, 6 + channel), (SIDE, BLOCK)) for channel in range(3)
            ]
            for row in range(SIDE):
                start = tile * TILE + row * SIDE
                before = carry_ref[tile, row_of(row)]
                weight = alpha_ref[tile, layer, row_of(row)] * jnp.exp(
                    sums[start : start + SIDE, :BLOCK] + before
                )
                weight_ref[tile, layer, row_of(row)] = weight
                carry_ref[tile, row_of(row)] = before + sums[start : start + SIDE, BLOCK:]
                for channel in range(3):
                    color_ref[tile, channel, row_of(row)] += weight * shades[channel]
        return carry

    lax.fori_loop(0, LIST, forward, 0)

    for tile in range(tiles):
        goals = jnp.concatenate([goal_ref[tile], jnp.zeros((5, TILE), f32)], axis=0).T
        for channel in range(3):
            high, low = halves(color_ref[tile, channel], 2)
            color = jnp.dot(
                jnp.concatenate([high, low], axis=1), ones, preferred_element_type=f32
            )
            error = color - goals[:, channel : channel + 1]
            slope_ref[tile, channel] = error * lax.rsqrt(error * error + SMOOTHING) * (1.0 / 3.0)
    carry_ref[...] = jnp.zeros_like(carry_ref)

    def backward(step, carry):
        layer = LIST - 1 - step
        color_grads = []
        for tile in range(tiles):
            slot = jnp.maximum(lists_ref[tile * LIST + layer], 0)
            shades = [
                jnp.broadcast_to(feature(slot, 6 + channel), (SIDE, BLOCK)) for channel in range(3)
            ]
            grads = [jnp.zeros((SIDE, BLOCK), f32) for _ in range(3)]
            for row in range(SIDE):
                weight = weight_ref[tile, layer, row_of(row)]
                pulled = [weight * slope_ref[tile, channel, row_of(row)] for channel in range(3)]
                grads = [grads[channel] + pulled[channel] for channel in range(3)]
                gain = (
                    pulled[0] * shades[0] + pulled[1] * shades[1] + pulled[2] * shades[2]
                )
                weight_ref[tile, layer, row_of(row)] = gain
                high, low = halves(gain, 2)
                start = tile * TILE + row * SIDE
                pieces_ref[start : start + SIDE, :BLOCK] = high
                pieces_ref[start : start + SIDE, BLOCK:] = low
            color_grads.append([jnp.sum(grad, axis=0, keepdims=True) for grad in grads])
        sums = jnp.dot(pieces_ref[...], later, preferred_element_type=f32)
        for tile in range(tiles):
            entry = lists_ref[tile * LIST + layer]
            slot = jnp.maximum(entry, 0)
            middle_x, middle_y = center(tile)
            delta_x = column - (feature(slot, 0) - middle_x)
            place_y = jnp.broadcast_to(feature(slot, 1) - middle_y, (SIDE, BLOCK))
            flat = jnp.zeros((SIDE, BLOCK), f32)
            tilt = jnp.zeros((SIDE, BLOCK), f32)
            bend = jnp.zeros((SIDE, BLOCK), f32)
            for row in range(SIDE):
                start = tile * TILE + row * SIDE
                alpha = alpha_ref[tile, layer, row_of(row)]
                after = carry_ref[tile, row_of(row)]
                behind = sums[start : start + SIDE, :BLOCK] + after
                carry_ref[tile, row_of(row)] = after + sums[start : start + SIDE, BLOCK:]
                power_grad = weight_ref[tile, layer, row_of(row)] - behind * (
                    alpha / (1.0 - alpha)
                )
                delta_y = (row - (SIDE / 2 - 0.5)) - place_y
                turned = power_grad * delta_y
                flat += power_grad
                tilt += turned
                bend += turned * delta_y

            def total(values):
                return jnp.sum(values, axis=0, keepdims=True)

            sum_x = total(flat * delta_x)
            sum_y = total(tilt)
            conic_a, conic_b, conic_c = feature(slot, 2), feature(slot, 3), feature(slot, 4)
            results = [
                conic_a * sum_x + conic_b * sum_y,
                conic_b * sum_x + conic_c * sum_y,
                -0.5 * total(flat * delta_x * delta_x),
                -total(tilt * delta_x),
                -0.5 * total(bend),
                total(flat),
            ] + color_grads[tile]

            @pl.when(entry >= 0)
            def _():
                for index in range(FEATS):
                    out_ref[slot, :, index * BLOCK : (index + 1) * BLOCK] = results[index]

        return carry

    lax.fori_loop(0, LIST, backward, 0)


def collect_kernel(keys_ref, slots_ref, out_ref):
    count, width = out_ref.shape[0], slots_ref.shape[0]
    wanted = lax.broadcasted_iota(jnp.int32, (count, width), 0)
    picker = jnp.where(keys_ref[...] == wanted, 1.0, 0.0).astype(jnp.bfloat16)
    total = jnp.zeros(out_ref.shape, jnp.float32)
    for piece in halves(slots_ref[...], 3):
        total += jnp.dot(picker, piece, preferred_element_type=jnp.float32)
    out_ref[...] = total


def update_kernel(
    blocks_here,
    center_x,
    center_y,
    cot_ref,
    params_ref,
    adam_m_ref,
    adam_v_ref,
    new_params_ref,
    new_m_ref,
    new_v_ref,
    grad_ref,
):
    codes = 2 * blocks_here
    rows = code_rows(params_ref, blocks_here)
    shift = code_shift(blocks_here)
    cots = [cot_ref[codes * feat : codes * (feat + 1)] for feat in range(FEATS)]
    used = rows[:10] + rows[11:]

    def shown_of(values):
        return project(values[:10] + [None] + values[10:], shift, center_x, center_y)

    _, pull = jax.vjp(shown_of, used)
    grads = pull(cots[:5] + cots[6:])[0]
    logit_grad = cots[5] * (1.0 - jax.nn.sigmoid(rows[10]))
    grads = grads[:10] + [logit_grad] + grads[10:]
    for row in range(PARAMS):
        both = grads[row][:blocks_here] + grads[row][blocks_here:]
        for block in range(blocks_here):
            grad_ref[row : row + 1, block * BLOCK : (block + 1) * BLOCK] = both[block : block + 1]
    grad = grad_ref[...]
    new_m = BETA_ONE * adam_m_ref[...] + (1.0 - BETA_ONE) * grad
    new_v = BETA_TWO * adam_v_ref[...] + (1.0 - BETA_TWO) * grad * grad
    m_hat = new_m * (1.0 / (1.0 - BETA_ONE**ADAM_STEP))
    v_hat = new_v * (1.0 / (1.0 - BETA_TWO**ADAM_STEP))
    row = lax.broadcasted_iota(jnp.int32, grad.shape, 0)
    rates = jnp.full(grad.shape, RATES[0][1], jnp.float32)
    for first, rate in RATES[1:]:
        rates = jnp.where(row >= first, jnp.float32(rate), rates)
    new_params_ref[...] = params_ref[...] - rates * m_hat / (jnp.sqrt(v_hat) + ADAM_EPS)
    new_m_ref[...] = new_m
    new_v_ref[...] = new_v


def vmem(count):
    return [pl.BlockSpec(memory_space=VMEM)] * count


def smem(count):
    return [pl.BlockSpec(memory_space=SMEM)] * count


def on_device(params, adam_m, adam_v, target, tile_ids, send_blocks, tile_lists):
    dev_count = lax.axis_size("dev")
    g_local = params.shape[1]
    blocks_here = g_local // BLOCK
    codes = 2 * blocks_here
    tiles_y = dev_count * blocks_here // TILES_X
    center_x = 8.0 * TILES_X
    center_y = 8.0 * tiles_y
    tiles = tile_ids.shape[2]
    f32 = jnp.float32
    limit = pltpu.CompilerParams(vmem_limit_bytes=VMEM_LIMIT)
    provided = send_blocks.reshape(-1)
    slot_shape = jax.ShapeDtypeStruct((dev_count, 1, SLOT), f32)

    outgoing = pl.pallas_call(
        lambda *refs: project_kernel(blocks_here, center_x, center_y, *refs),
        out_shape=slot_shape,
        in_specs=smem(1) + vmem(1),
        out_specs=vmem(1)[0],
        scratch_shapes=[pltpu.VMEM((codes, 1, SLOT), f32)],
        compiler_params=limit,
        name="project",
    )(provided, params)
    incoming = lax.all_to_all(outgoing, "dev", split_axis=0, concat_axis=0, tiled=True)
    pairs = pltpu.VMEM((tiles, LIST, TILE, BLOCK), f32)
    cotangent = pl.pallas_call(
        lambda *refs: render_kernel(tiles_y, *refs),
        out_shape=slot_shape,
        in_specs=smem(2) + vmem(2),
        out_specs=vmem(1)[0],
        scratch_shapes=[
            pairs,
            pairs,
            pltpu.VMEM((tiles * TILE, 2 * BLOCK), jnp.bfloat16),
            pltpu.VMEM((tiles, TILE, BLOCK), f32),
            pltpu.VMEM((tiles, 3, TILE, BLOCK), f32),
            pltpu.VMEM((tiles, 3, TILE, BLOCK), f32),
        ],
        compiler_params=limit,
        name="render",
    )(tile_ids.reshape(-1), tile_lists.reshape(-1), incoming, target.reshape(target.shape[2:]))
    returned = lax.all_to_all(cotangent, "dev", split_axis=0, concat_axis=0, tiled=True)
    order = jnp.arange(FEATS, dtype=jnp.int32) * codes
    keys = jnp.where(provided[:, None] >= 0, provided[:, None] + order[None, :], -1)
    per_code = pl.pallas_call(
        collect_kernel,
        out_shape=jax.ShapeDtypeStruct((FEATS * codes, BLOCK), f32),
        in_specs=vmem(2),
        out_specs=vmem(1)[0],
        compiler_params=limit,
        name="collect",
    )(keys.reshape(1, dev_count * FEATS), returned.reshape(dev_count * FEATS, BLOCK))
    per_code = lax.psum(per_code, "rep")
    shape = jax.ShapeDtypeStruct(params.shape, f32)
    return pl.pallas_call(
        lambda *refs: update_kernel(blocks_here, center_x, center_y, *refs),
        out_shape=(shape,) * 4,
        in_specs=vmem(4),
        out_specs=tuple(vmem(4)),
        compiler_params=limit,
        name="update",
    )(per_code, params, adam_m, adam_v)


def solution(mesh):
    placed = (
        P(None, "dev"),
        P(None, "dev"),
        P(None, "dev"),
        P("rep", "dev", None, None, None),
        P("rep", "dev", None),
        P("rep", "dev", None, None),
        P("rep", "dev", None, None),
    )
    return jax.shard_map(
        on_device,
        mesh=mesh,
        in_specs=placed,
        out_specs=(P(None, "dev"), P(None, "dev"), P(None, "dev"), P(None, "dev")),
        check_vma=False,
    )
```

```python
import jax
import jax.numpy as jnp
from jax import lax
from jax.experimental import pallas as pl
from jax.experimental.pallas import tpu as pltpu
from jax.sharding import PartitionSpec as P

BLOCK = 128
PARAMS = 59
FEATS = 9
SLOT = FEATS * BLOCK
TILE = 256
SIDE = 16
LIST = 8
TILES_X = 64
ADAM_STEP = 1000

FOCAL = 1100.0
DEPTH_ZERO = 20.0
BASELINE = 16.0 * DEPTH_ZERO / FOCAL
BLUR = 0.3
SMOOTHING = 0.0001
BETA_ONE = 0.9
BETA_TWO = 0.999
ADAM_EPS = 1e-15
SH_ZERO = 0.28209479177387814
SH_ONE = 0.4886025119029199
SH_TWO = [
    1.0925484305920792,
    -1.0925484305920792,
    0.31539156525252005,
    -1.0925484305920792,
    0.5462742152960396,
]
SH_THREE = [
    -0.5900435899266435,
    2.890611442640554,
    -0.4570457994644658,
    0.3731763325901154,
    -0.4570457994644658,
    1.445305721320277,
    -0.5900435899266435,
]
RATES = [(0, 0.00016), (3, 0.005), (6, 0.001), (10, 0.05), (11, 0.0025), (14, 0.000125)]

VMEM_LIMIT = 40 * 1024 * 1024
SMEM = pltpu.MemorySpace.SMEM
VMEM = pltpu.MemorySpace.VMEM


def sh_basis(unit_x, unit_y, unit_z):
    square_x = unit_x * unit_x
    square_y = unit_y * unit_y
    square_z = unit_z * unit_z
    return [
        SH_ZERO + 0.0 * unit_x,
        -SH_ONE * unit_y,
        SH_ONE * unit_z,
        -SH_ONE * unit_x,
        SH_TWO[0] * unit_x * unit_y,
        SH_TWO[1] * unit_y * unit_z,
        SH_TWO[2] * (2.0 * square_z - square_x - square_y),
        SH_TWO[3] * unit_x * unit_z,
        SH_TWO[4] * (square_x - square_y),
        SH_THREE[0] * unit_y * (3.0 * square_x - square_y),
        SH_THREE[1] * unit_x * unit_y * unit_z,
        SH_THREE[2] * unit_y * (4.0 * square_z - square_x - square_y),
        SH_THREE[3] * unit_z * (2.0 * square_z - 3.0 * square_x - 3.0 * square_y),
        SH_THREE[4] * unit_x * (4.0 * square_z - square_x - square_y),
        SH_THREE[5] * unit_z * (square_x - square_y),
        SH_THREE[6] * unit_x * (square_x - 3.0 * square_y),
    ]


def project(rows, shift, center_x, center_y):
    offset_x = rows[0] - shift
    offset_y = rows[1]
    depth = rows[2]
    inverse = 1.0 / depth
    focal_depth = FOCAL * inverse
    screen_x = focal_depth * offset_x + center_x
    screen_y = focal_depth * offset_y + center_y
    scales = [jnp.exp(rows[3 + index]) for index in range(3)]
    norm = jnp.sqrt(
        rows[6] * rows[6] + rows[7] * rows[7] + rows[8] * rows[8] + rows[9] * rows[9]
    )
    quat_w, quat_x, quat_y, quat_z = [rows[6 + index] / norm for index in range(4)]
    rotation = [
        [
            1.0 - 2.0 * (quat_y * quat_y + quat_z * quat_z),
            2.0 * (quat_x * quat_y - quat_w * quat_z),
            2.0 * (quat_x * quat_z + quat_w * quat_y),
        ],
        [
            2.0 * (quat_x * quat_y + quat_w * quat_z),
            1.0 - 2.0 * (quat_x * quat_x + quat_z * quat_z),
            2.0 * (quat_y * quat_z - quat_w * quat_x),
        ],
        [
            2.0 * (quat_x * quat_z - quat_w * quat_y),
            2.0 * (quat_y * quat_z + quat_w * quat_x),
            1.0 - 2.0 * (quat_x * quat_x + quat_y * quat_y),
        ],
    ]
    slope_x = focal_depth * offset_x * inverse
    slope_y = focal_depth * offset_y * inverse
    first_row = [
        (focal_depth * rotation[0][index] - slope_x * rotation[2][index]) * scales[index]
        for index in range(3)
    ]
    second_row = [
        (focal_depth * rotation[1][index] - slope_y * rotation[2][index]) * scales[index]
        for index in range(3)
    ]
    sigma_xx = (
        first_row[0] * first_row[0]
        + first_row[1] * first_row[1]
        + first_row[2] * first_row[2]
        + BLUR
    )
    sigma_xy = (
        first_row[0] * second_row[0] + first_row[1] * second_row[1] + first_row[2] * second_row[2]
    )
    sigma_yy = (
        second_row[0] * second_row[0]
        + second_row[1] * second_row[1]
        + second_row[2] * second_row[2]
        + BLUR
    )
    determinant = sigma_xx * sigma_yy - sigma_xy * sigma_xy
    distance = jnp.sqrt(offset_x * offset_x + offset_y * offset_y + depth * depth)
    basis = sh_basis(offset_x / distance, offset_y / distance, depth / distance)
    colors = []
    for channel in range(3):
        total = basis[0] * rows[11 + channel]
        for index in range(1, 16):
            total = total + basis[index] * rows[11 + 3 * index + channel]
        colors.append(jnp.maximum(total + 0.5, 0.0))
    return [
        screen_x,
        screen_y,
        sigma_yy / determinant,
        -sigma_xy / determinant,
        sigma_xx / determinant,
        colors[0],
        colors[1],
        colors[2],
    ]


def code_rows(params_ref, blocks_here):
    rows = []
    for row in range(PARAMS):
        parts = [
            params_ref[row : row + 1, block * BLOCK : (block + 1) * BLOCK]
            for block in range(blocks_here)
        ]
        rows.append(jnp.concatenate(parts + parts, axis=0))
    return rows


def code_shift(blocks_here):
    code = lax.broadcasted_iota(jnp.int32, (2 * blocks_here, BLOCK), 0)
    return jnp.where(code >= blocks_here, BASELINE, 0.0).astype(jnp.float32)


def halves(values, pieces):
    out = []
    rest = values
    for index in range(pieces):
        part = rest.astype(jnp.bfloat16)
        out.append(part)
        if index < pieces - 1:
            rest = rest - part.astype(jnp.float32)
    return out


def project_kernel(
    blocks_here, center_x, center_y, codes_hbm, params_hbm, out_ref, codes_ref, params_ref, table_ref, sems
):
    copies = [
        pltpu.make_async_copy(params_hbm, params_ref, sems.at[0]),
        pltpu.make_async_copy(codes_hbm, codes_ref, sems.at[1]),
    ]
    for copy in copies:
        copy.start()
    copies[0].wait()
    rows = code_rows(params_ref, blocks_here)
    shown = project(rows, code_shift(blocks_here), center_x, center_y)
    shown = shown[:5] + [jax.nn.sigmoid(rows[10])] + shown[5:]
    for code in range(2 * blocks_here):
        for feat in range(FEATS):
            table_ref[code, feat : feat + 1] = shown[feat][code : code + 1]
    copies[1].wait()

    def fill(target, carry):
        code = jnp.maximum(codes_ref[target], 0)
        out_ref[pl.ds(target * FEATS, 8)] = table_ref[code, 0:8]
        out_ref[pl.ds(target * FEATS + 8, 1)] = table_ref[code, 8:9]
        return carry

    lax.fori_loop(0, out_ref.shape[0] // FEATS, fill, 0, unroll=8)


def render_kernel(
    tiles_y,
    scalars_ref,
    slots_ref,
    goal_ref,
    out_ref,
    alpha_ref,
    weight_ref,
    pieces_ref,
    carry_ref,
    color_ref,
    slope_ref,
):
    tiles = goal_ref.shape[0]
    per_view = TILES_X * tiles_y
    f32 = jnp.float32
    half = SIDE // 2
    lane = lax.broadcasted_iota(jnp.int32, (2 * BLOCK, 2 * BLOCK), 1)
    depth = lax.broadcasted_iota(jnp.int32, (2 * BLOCK, 2 * BLOCK), 0) % BLOCK
    earlier = jnp.where((lane >= BLOCK) | (depth < lane), 1.0, 0.0).astype(jnp.bfloat16)
    later = jnp.where((lane >= BLOCK) | (depth > lane), 1.0, 0.0).astype(jnp.bfloat16)
    ones = jnp.ones((2 * BLOCK, BLOCK), jnp.bfloat16)
    column = lax.broadcasted_iota(jnp.int32, (half, BLOCK), 0).astype(f32) - (SIDE / 2 - 0.5)

    out_ref[...] = jnp.zeros_like(out_ref)

    def entry_of(tile, layer):
        return scalars_ref[tiles + tile * LIST + layer]

    def feature(slot, index):
        return slots_ref[pl.ds(slot * FEATS + index, 1)]

    def wide(row):
        return jnp.broadcast_to(row, (half, BLOCK))

    def center(tile):
        within = lax.rem(scalars_ref[tile], per_view)
        middle_x = (lax.rem(within, TILES_X) * SIDE + half).astype(f32)
        middle_y = (lax.div(within, TILES_X) * SIDE + half).astype(f32)
        return middle_x, middle_y

    def row_of(index, part):
        start = index * SIDE + part * half
        return slice(start, start + half)

    def offsets(tile, slot):
        middle_x, middle_y = center(tile)
        place_x = wide(feature(slot, 0) - middle_x)
        place_y = wide(feature(slot, 1) - middle_y)
        return [column + part * half - place_x for part in range(2)], place_y

    def split_row(tile, row, parts):
        pairs = [halves(part, 2) for part in parts]
        start = tile * TILE + row * SIDE
        for side in range(2):
            both = jnp.concatenate([pair[side] for pair in pairs], axis=0)
            pieces_ref[start : start + SIDE, side * BLOCK : (side + 1) * BLOCK] = both

    def add_up(matrix):
        return jnp.dot(pieces_ref[...], matrix, preferred_element_type=f32)

    def forward(layer, carry):
        for tile in range(tiles):
            entry = entry_of(tile, layer)
            slot = jnp.maximum(entry, 0)
            live = jnp.where(entry >= 0, 1.0, 0.0).astype(f32)
            delta_x, place_y = offsets(tile, slot)
            half_x = [wide(-0.5 * feature(slot, 2)) * delta * delta for delta in delta_x]
            cross = [wide(-feature(slot, 3)) * delta for delta in delta_x]
            half_y = wide(-0.5 * feature(slot, 4))
            opacity = wide(feature(slot, 5) * live)
            for row in range(SIDE):
                delta_y = (row - (SIDE / 2 - 0.5)) - place_y
                scaled_y = half_y * delta_y
                logs = []
                for part in range(2):
                    power = half_x[part] + delta_y * (cross[part] + scaled_y)
                    alpha = opacity * jnp.exp(power)
                    alpha_ref[tile, layer, row_of(row, part)] = alpha
                    logs.append(jnp.log(1.0 - alpha))
                split_row(tile, row, logs)
        sums = add_up(earlier)
        for tile in range(tiles):
            slot = jnp.maximum(entry_of(tile, layer), 0)
            shades = [wide(feature(slot, 6 + channel)) for channel in range(3)]
            for row in range(SIDE):
                for part in range(2):
                    where = row_of(row, part)
                    start = tile * TILE + where.start
                    before = carry_ref[tile, where]
                    weight = alpha_ref[tile, layer, where] * jnp.exp(
                        sums[start : start + half, :BLOCK] + before
                    )
                    weight_ref[tile, layer, where] = weight
                    carry_ref[tile, where] = before + sums[start : start + half, BLOCK:]
                    for channel in range(3):
                        color_ref[tile, channel, where] += weight * shades[channel]
        return carry

    color_ref[...] = jnp.zeros_like(color_ref)
    carry_ref[...] = jnp.zeros_like(carry_ref)
    lax.fori_loop(0, LIST, forward, 0, unroll=8)

    for tile in range(tiles):
        goals = jnp.concatenate([goal_ref[tile], jnp.zeros((5, TILE), f32)], axis=0).T
        for channel in range(3):
            high, low = halves(color_ref[tile, channel], 2)
            color = jnp.dot(
                jnp.concatenate([high, low], axis=1), ones, preferred_element_type=f32
            )
            error = color - goals[:, channel : channel + 1]
            slope_ref[tile, channel] = error * lax.rsqrt(error * error + SMOOTHING) * (1.0 / 3.0)
    carry_ref[...] = jnp.zeros_like(carry_ref)

    def total(values):
        return jnp.sum(values, axis=0, keepdims=True)

    def backward(step, carry):
        layer = LIST - 1 - step
        color_grads = []
        for tile in range(tiles):
            slot = jnp.maximum(entry_of(tile, layer), 0)
            shades = [wide(feature(slot, 6 + channel)) for channel in range(3)]
            grads = [jnp.zeros((half, BLOCK), f32) for _ in range(3)]
            for row in range(SIDE):
                parts = []
                for part in range(2):
                    where = row_of(row, part)
                    weight = weight_ref[tile, layer, where]
                    pulled = [weight * slope_ref[tile, channel, where] for channel in range(3)]
                    grads = [grads[channel] + pulled[channel] for channel in range(3)]
                    gain = pulled[0] * shades[0] + pulled[1] * shades[1] + pulled[2] * shades[2]
                    weight_ref[tile, layer, where] = gain
                    parts.append(gain)
                split_row(tile, row, parts)
            color_grads.append([total(grad) for grad in grads])
        sums = add_up(later)
        for tile in range(tiles):
            slot = jnp.maximum(entry_of(tile, layer), 0)
            delta_x, place_y = offsets(tile, slot)
            flat = [jnp.zeros((half, BLOCK), f32) for _ in range(2)]
            tilt = [jnp.zeros((half, BLOCK), f32) for _ in range(2)]
            bend = jnp.zeros((half, BLOCK), f32)
            for row in range(SIDE):
                delta_y = (row - (SIDE / 2 - 0.5)) - place_y
                for part in range(2):
                    where = row_of(row, part)
                    start = tile * TILE + where.start
                    alpha = alpha_ref[tile, layer, where]
                    after = carry_ref[tile, where]
                    behind = sums[start : start + half, :BLOCK] + after
                    carry_ref[tile, where] = after + sums[start : start + half, BLOCK:]
                    power_grad = weight_ref[tile, layer, where] - behind * (alpha / (1.0 - alpha))
                    turned = power_grad * delta_y
                    flat[part] += power_grad
                    tilt[part] += turned
                    bend += turned * delta_y
            leaned = [flat[part] * delta_x[part] for part in range(2)]
            sum_x = total(leaned[0] + leaned[1])
            sum_y = total(tilt[0] + tilt[1])
            conic_a, conic_b, conic_c = feature(slot, 2), feature(slot, 3), feature(slot, 4)
            results = [
                conic_a * sum_x + conic_b * sum_y,
                conic_b * sum_x + conic_c * sum_y,
                -0.5 * total(leaned[0] * delta_x[0] + leaned[1] * delta_x[1]),
                -total(tilt[0] * delta_x[0] + tilt[1] * delta_x[1]),
                -0.5 * total(bend),
                total(flat[0] + flat[1]),
            ] + color_grads[tile]
            for index in range(FEATS):
                out_ref[pl.ds(slot * FEATS + index, 1)] += results[index]
        return carry

    lax.fori_loop(0, LIST, backward, 0, unroll=8)


def collect_kernel(keys_ref, slots_ref, out_ref):
    count, width = out_ref.shape[0], slots_ref.shape[0]
    wanted = lax.broadcasted_iota(jnp.int32, (count, width), 0)
    picker = jnp.where(keys_ref[...] == wanted, 1.0, 0.0).astype(jnp.bfloat16)
    total = jnp.zeros(out_ref.shape, jnp.float32)
    for piece in halves(slots_ref[...], 3):
        total += jnp.dot(picker, piece, preferred_element_type=jnp.float32)
    out_ref[...] = total


def update_kernel(
    blocks_here,
    center_x,
    center_y,
    cot_ref,
    params_ref,
    adam_m_ref,
    adam_v_ref,
    new_params_ref,
    new_m_ref,
    new_v_ref,
    grad_ref,
):
    codes = 2 * blocks_here
    rows = code_rows(params_ref, blocks_here)
    shift = code_shift(blocks_here)
    summed = cot_ref[0]
    for group in range(1, cot_ref.shape[0]):
        summed = summed + cot_ref[group]
    cots = [summed[codes * feat : codes * (feat + 1)] for feat in range(FEATS)]
    used = rows[:10] + rows[11:]

    def shown_of(values):
        return project(values[:10] + [None] + values[10:], shift, center_x, center_y)

    _, pull = jax.vjp(shown_of, used)
    grads = pull(cots[:5] + cots[6:])[0]
    logit_grad = cots[5] * (1.0 - jax.nn.sigmoid(rows[10]))
    grads = grads[:10] + [logit_grad] + grads[10:]
    for row in range(PARAMS):
        both = grads[row][:blocks_here] + grads[row][blocks_here:]
        for block in range(blocks_here):
            grad_ref[row : row + 1, block * BLOCK : (block + 1) * BLOCK] = both[block : block + 1]
    grad = grad_ref[...]
    new_m = BETA_ONE * adam_m_ref[...] + (1.0 - BETA_ONE) * grad
    new_v = BETA_TWO * adam_v_ref[...] + (1.0 - BETA_TWO) * grad * grad
    m_hat = new_m * (1.0 / (1.0 - BETA_ONE**ADAM_STEP))
    v_hat = new_v * (1.0 / (1.0 - BETA_TWO**ADAM_STEP))
    row = lax.broadcasted_iota(jnp.int32, grad.shape, 0)
    rates = jnp.full(grad.shape, RATES[0][1], jnp.float32)
    for first, rate in RATES[1:]:
        rates = jnp.where(row >= first, jnp.float32(rate), rates)
    new_params_ref[...] = params_ref[...] - rates * m_hat / (jnp.sqrt(v_hat) + ADAM_EPS)
    new_m_ref[...] = new_m
    new_v_ref[...] = new_v


def vmem(count):
    return [pl.BlockSpec(memory_space=VMEM)] * count


def smem(count):
    return [pl.BlockSpec(memory_space=SMEM)] * count


def run_project(params, provided, center_x, center_y, limit):
    blocks_here = params.shape[1] // BLOCK
    codes = 2 * blocks_here
    f32 = jnp.float32
    return pl.pallas_call(
        lambda *refs: project_kernel(blocks_here, center_x, center_y, *refs),
        out_shape=jax.ShapeDtypeStruct((provided.shape[0] * FEATS, BLOCK), f32),
        in_specs=[pl.BlockSpec(memory_space=pltpu.MemorySpace.HBM)] * 2,
        out_specs=vmem(1)[0],
        scratch_shapes=[
            pltpu.SMEM(provided.shape, jnp.int32),
            pltpu.VMEM(params.shape, f32),
            pltpu.VMEM((codes, FEATS, BLOCK), f32),
            pltpu.SemaphoreType.DMA((2,)),
        ],
        compiler_params=limit,
        name="project",
    )(provided, params)


def run_render(scalars, incoming, goals, tiles_y, limit):
    tiles = goals.shape[0]
    f32 = jnp.float32
    pairs = pltpu.VMEM((tiles, LIST, TILE, BLOCK), f32)
    return pl.pallas_call(
        lambda *refs: render_kernel(tiles_y, *refs),
        out_shape=jax.ShapeDtypeStruct(incoming.shape, f32),
        in_specs=smem(1) + vmem(2),
        out_specs=vmem(1)[0],
        scratch_shapes=[
            pairs,
            pairs,
            pltpu.VMEM((tiles * TILE, 2 * BLOCK), jnp.bfloat16),
            pltpu.VMEM((tiles, TILE, BLOCK), f32),
            pltpu.VMEM((tiles, 3, TILE, BLOCK), f32),
            pltpu.VMEM((tiles, 3, TILE, BLOCK), f32),
        ],
        compiler_params=limit,
        name="render",
    )(scalars, incoming, goals)


def run_collect(keys, returned, codes, limit):
    return pl.pallas_call(
        collect_kernel,
        out_shape=jax.ShapeDtypeStruct((FEATS * codes, BLOCK), jnp.float32),
        in_specs=vmem(2),
        out_specs=vmem(1)[0],
        compiler_params=limit,
        name="collect",
    )(keys, returned)


def run_update(gathered, params, adam_m, adam_v, center_x, center_y, limit):
    blocks_here = params.shape[1] // BLOCK
    shape = jax.ShapeDtypeStruct(params.shape, jnp.float32)
    return pl.pallas_call(
        lambda *refs: update_kernel(blocks_here, center_x, center_y, *refs),
        out_shape=(shape,) * 4,
        in_specs=vmem(4),
        out_specs=tuple(vmem(4)),
        compiler_params=limit,
        name="update",
    )(gathered, params, adam_m, adam_v)


def exchange(slots, dev_count):
    sent = slots.reshape(dev_count, 1, SLOT)
    return lax.all_to_all(sent, "dev", split_axis=0, concat_axis=0, tiled=True).reshape(slots.shape)


def on_device(params, adam_m, adam_v, target, tile_ids, send_blocks, tile_lists):
    dev_count = lax.axis_size("dev")
    blocks_here = params.shape[1] // BLOCK
    codes = 2 * blocks_here
    tiles_y = dev_count * blocks_here // TILES_X
    center_x = 8.0 * TILES_X
    center_y = 8.0 * tiles_y
    limit = pltpu.CompilerParams(vmem_limit_bytes=VMEM_LIMIT)
    provided = send_blocks.reshape(-1)
    scalars = jnp.concatenate([tile_ids.reshape(-1), tile_lists.reshape(-1)])

    outgoing = run_project(params, provided, center_x, center_y, limit)
    incoming = exchange(outgoing, dev_count)
    goals = target.reshape(target.shape[2:])
    cotangent = run_render(scalars, incoming, goals, tiles_y, limit)
    returned = exchange(cotangent, dev_count)
    order = jnp.arange(FEATS, dtype=jnp.int32) * codes
    keys = jnp.where(provided[:, None] >= 0, provided[:, None] + order[None, :], -1)
    per_code = run_collect(keys.reshape(1, dev_count * FEATS), returned, codes, limit)
    gathered = lax.all_gather(per_code, "rep", axis=0, tiled=False)
    return run_update(gathered, params, adam_m, adam_v, center_x, center_y, limit)


def solution(mesh):
    placed = (
        P(None, "dev"),
        P(None, "dev"),
        P(None, "dev"),
        P("rep", "dev", None, None, None),
        P("rep", "dev", None),
        P("rep", "dev", None, None),
        P("rep", "dev", None, None),
    )
    return jax.shard_map(
        on_device,
        mesh=mesh,
        in_specs=placed,
        out_specs=(P(None, "dev"), P(None, "dev"), P(None, "dev"), P(None, "dev")),
        check_vma=False,
    )
```

```python
import jax
import jax.numpy as jnp
from jax import lax
from jax.experimental import pallas as pl
from jax.experimental.pallas import tpu as pltpu
from jax.sharding import PartitionSpec as P

BLOCK = 128
PARAMS = 59
FEATS = 9
SLOT = FEATS * BLOCK
TILE = 256
SIDE = 16
LIST = 8
TILES_X = 64
ADAM_STEP = 1000

FOCAL = 1100.0
DEPTH_ZERO = 20.0
BASELINE = 16.0 * DEPTH_ZERO / FOCAL
BLUR = 0.3
SMOOTHING = 0.0001
BETA_ONE = 0.9
BETA_TWO = 0.999
ADAM_EPS = 1e-15
SH_ZERO = 0.28209479177387814
SH_ONE = 0.4886025119029199
SH_TWO = [
    1.0925484305920792,
    -1.0925484305920792,
    0.31539156525252005,
    -1.0925484305920792,
    0.5462742152960396,
]
SH_THREE = [
    -0.5900435899266435,
    2.890611442640554,
    -0.4570457994644658,
    0.3731763325901154,
    -0.4570457994644658,
    1.445305721320277,
    -0.5900435899266435,
]
RATES = [(0, 0.00016), (3, 0.005), (6, 0.001), (10, 0.05), (11, 0.0025), (14, 0.000125)]

VMEM_LIMIT = 40 * 1024 * 1024
WHOLE_VMEM = 60 * 1024 * 1024
SMEM = pltpu.MemorySpace.SMEM
VMEM = pltpu.MemorySpace.VMEM


def sh_basis(unit_x, unit_y, unit_z):
    square_x = unit_x * unit_x
    square_y = unit_y * unit_y
    square_z = unit_z * unit_z
    return [
        SH_ZERO + 0.0 * unit_x,
        -SH_ONE * unit_y,
        SH_ONE * unit_z,
        -SH_ONE * unit_x,
        SH_TWO[0] * unit_x * unit_y,
        SH_TWO[1] * unit_y * unit_z,
        SH_TWO[2] * (2.0 * square_z - square_x - square_y),
        SH_TWO[3] * unit_x * unit_z,
        SH_TWO[4] * (square_x - square_y),
        SH_THREE[0] * unit_y * (3.0 * square_x - square_y),
        SH_THREE[1] * unit_x * unit_y * unit_z,
        SH_THREE[2] * unit_y * (4.0 * square_z - square_x - square_y),
        SH_THREE[3] * unit_z * (2.0 * square_z - 3.0 * square_x - 3.0 * square_y),
        SH_THREE[4] * unit_x * (4.0 * square_z - square_x - square_y),
        SH_THREE[5] * unit_z * (square_x - square_y),
        SH_THREE[6] * unit_x * (square_x - 3.0 * square_y),
    ]


def project(rows, shift, center_x, center_y):
    offset_x = rows[0] - shift
    offset_y = rows[1]
    depth = rows[2]
    inverse = 1.0 / depth
    focal_depth = FOCAL * inverse
    screen_x = focal_depth * offset_x + center_x
    screen_y = focal_depth * offset_y + center_y
    scales = [jnp.exp(rows[3 + index]) for index in range(3)]
    norm = jnp.sqrt(
        rows[6] * rows[6] + rows[7] * rows[7] + rows[8] * rows[8] + rows[9] * rows[9]
    )
    quat_w, quat_x, quat_y, quat_z = [rows[6 + index] / norm for index in range(4)]
    rotation = [
        [
            1.0 - 2.0 * (quat_y * quat_y + quat_z * quat_z),
            2.0 * (quat_x * quat_y - quat_w * quat_z),
            2.0 * (quat_x * quat_z + quat_w * quat_y),
        ],
        [
            2.0 * (quat_x * quat_y + quat_w * quat_z),
            1.0 - 2.0 * (quat_x * quat_x + quat_z * quat_z),
            2.0 * (quat_y * quat_z - quat_w * quat_x),
        ],
        [
            2.0 * (quat_x * quat_z - quat_w * quat_y),
            2.0 * (quat_y * quat_z + quat_w * quat_x),
            1.0 - 2.0 * (quat_x * quat_x + quat_y * quat_y),
        ],
    ]
    slope_x = focal_depth * offset_x * inverse
    slope_y = focal_depth * offset_y * inverse
    first_row = [
        (focal_depth * rotation[0][index] - slope_x * rotation[2][index]) * scales[index]
        for index in range(3)
    ]
    second_row = [
        (focal_depth * rotation[1][index] - slope_y * rotation[2][index]) * scales[index]
        for index in range(3)
    ]
    sigma_xx = (
        first_row[0] * first_row[0]
        + first_row[1] * first_row[1]
        + first_row[2] * first_row[2]
        + BLUR
    )
    sigma_xy = (
        first_row[0] * second_row[0] + first_row[1] * second_row[1] + first_row[2] * second_row[2]
    )
    sigma_yy = (
        second_row[0] * second_row[0]
        + second_row[1] * second_row[1]
        + second_row[2] * second_row[2]
        + BLUR
    )
    determinant = sigma_xx * sigma_yy - sigma_xy * sigma_xy
    distance = jnp.sqrt(offset_x * offset_x + offset_y * offset_y + depth * depth)
    basis = sh_basis(offset_x / distance, offset_y / distance, depth / distance)
    colors = []
    for channel in range(3):
        total = basis[0] * rows[11 + channel]
        for index in range(1, 16):
            total = total + basis[index] * rows[11 + 3 * index + channel]
        colors.append(jnp.maximum(total + 0.5, 0.0))
    return [
        screen_x,
        screen_y,
        sigma_yy / determinant,
        -sigma_xy / determinant,
        sigma_xx / determinant,
        colors[0],
        colors[1],
        colors[2],
    ]


def code_rows(params_ref, blocks_here):
    rows = []
    for row in range(PARAMS):
        parts = [
            params_ref[row : row + 1, block * BLOCK : (block + 1) * BLOCK]
            for block in range(blocks_here)
        ]
        rows.append(jnp.concatenate(parts + parts, axis=0))
    return rows


def code_shift(blocks_here):
    code = lax.broadcasted_iota(jnp.int32, (2 * blocks_here, BLOCK), 0)
    return jnp.where(code >= blocks_here, BASELINE, 0.0).astype(jnp.float32)


def halves(values, pieces):
    out = []
    rest = values
    for index in range(pieces):
        part = rest.astype(jnp.bfloat16)
        out.append(part)
        if index < pieces - 1:
            rest = rest - part.astype(jnp.float32)
    return out


def project_kernel(
    blocks_here, center_x, center_y, codes_hbm, params_hbm, out_ref, codes_ref, params_ref, table_ref, sems
):
    copies = [
        pltpu.make_async_copy(params_hbm, params_ref, sems.at[0]),
        pltpu.make_async_copy(codes_hbm, codes_ref, sems.at[1]),
    ]
    for copy in copies:
        copy.start()
    copies[0].wait()
    rows = code_rows(params_ref, blocks_here)
    shown = project(rows, code_shift(blocks_here), center_x, center_y)
    shown = shown[:5] + [jax.nn.sigmoid(rows[10])] + shown[5:]
    for code in range(2 * blocks_here):
        for feat in range(FEATS):
            table_ref[code, feat : feat + 1] = shown[feat][code : code + 1]
    copies[1].wait()

    def fill(target, carry):
        code = jnp.maximum(codes_ref[target], 0)
        out_ref[pl.ds(target * FEATS, 8)] = table_ref[code, 0:8]
        out_ref[pl.ds(target * FEATS + 8, 1)] = table_ref[code, 8:9]
        return carry

    lax.fori_loop(0, out_ref.shape[0] // FEATS, fill, 0, unroll=8)


def render_kernel(
    tiles_y,
    scalars_ref,
    slots_ref,
    goal_ref,
    out_ref,
    alpha_ref,
    weight_ref,
    pieces_ref,
    carry_ref,
    color_ref,
    slope_ref,
):
    tiles = goal_ref.shape[0]
    per_view = TILES_X * tiles_y
    f32 = jnp.float32
    half = SIDE // 2
    lane = lax.broadcasted_iota(jnp.int32, (2 * BLOCK, 2 * BLOCK), 1)
    depth = lax.broadcasted_iota(jnp.int32, (2 * BLOCK, 2 * BLOCK), 0) % BLOCK
    earlier = jnp.where((lane >= BLOCK) | (depth < lane), 1.0, 0.0).astype(jnp.bfloat16)
    later = jnp.where((lane >= BLOCK) | (depth > lane), 1.0, 0.0).astype(jnp.bfloat16)
    ones = jnp.ones((2 * BLOCK, BLOCK), jnp.bfloat16)
    column = lax.broadcasted_iota(jnp.int32, (half, BLOCK), 0).astype(f32) - (SIDE / 2 - 0.5)

    out_ref[...] = jnp.zeros_like(out_ref)

    def entry_of(tile, layer):
        return scalars_ref[tiles + tile * LIST + layer]

    def feature(slot, index):
        return slots_ref[pl.ds(slot * FEATS + index, 1)]

    def wide(row):
        return jnp.broadcast_to(row, (half, BLOCK))

    def center(tile):
        within = lax.rem(scalars_ref[tile], per_view)
        middle_x = (lax.rem(within, TILES_X) * SIDE + half).astype(f32)
        middle_y = (lax.div(within, TILES_X) * SIDE + half).astype(f32)
        return middle_x, middle_y

    def row_of(index, part):
        start = index * SIDE + part * half
        return slice(start, start + half)

    def offsets(tile, slot):
        middle_x, middle_y = center(tile)
        place_x = wide(feature(slot, 0) - middle_x)
        place_y = wide(feature(slot, 1) - middle_y)
        return [column + part * half - place_x for part in range(2)], place_y

    def split_row(tile, row, parts):
        pairs = [halves(part, 2) for part in parts]
        start = tile * TILE + row * SIDE
        for side in range(2):
            both = jnp.concatenate([pair[side] for pair in pairs], axis=0)
            pieces_ref[start : start + SIDE, side * BLOCK : (side + 1) * BLOCK] = both

    def add_up(matrix):
        return jnp.dot(pieces_ref[...], matrix, preferred_element_type=f32)

    def forward(layer, carry):
        for tile in range(tiles):
            entry = entry_of(tile, layer)
            slot = jnp.maximum(entry, 0)
            live = jnp.where(entry >= 0, 1.0, 0.0).astype(f32)
            delta_x, place_y = offsets(tile, slot)
            half_x = [wide(-0.5 * feature(slot, 2)) * delta * delta for delta in delta_x]
            cross = [wide(-feature(slot, 3)) * delta for delta in delta_x]
            half_y = wide(-0.5 * feature(slot, 4))
            opacity = wide(feature(slot, 5) * live)
            for row in range(SIDE):
                delta_y = (row - (SIDE / 2 - 0.5)) - place_y
                scaled_y = half_y * delta_y
                logs = []
                for part in range(2):
                    power = half_x[part] + delta_y * (cross[part] + scaled_y)
                    alpha = opacity * jnp.exp(power)
                    alpha_ref[tile, layer, row_of(row, part)] = alpha
                    logs.append(jnp.log(1.0 - alpha))
                split_row(tile, row, logs)
        sums = add_up(earlier)
        for tile in range(tiles):
            slot = jnp.maximum(entry_of(tile, layer), 0)
            shades = [wide(feature(slot, 6 + channel)) for channel in range(3)]
            for row in range(SIDE):
                for part in range(2):
                    where = row_of(row, part)
                    start = tile * TILE + where.start
                    before = carry_ref[tile, where]
                    weight = alpha_ref[tile, layer, where] * jnp.exp(
                        sums[start : start + half, :BLOCK] + before
                    )
                    weight_ref[tile, layer, where] = weight
                    carry_ref[tile, where] = before + sums[start : start + half, BLOCK:]
                    for channel in range(3):
                        color_ref[tile, channel, where] += weight * shades[channel]
        return carry

    color_ref[...] = jnp.zeros_like(color_ref)
    carry_ref[...] = jnp.zeros_like(carry_ref)
    lax.fori_loop(0, LIST, forward, 0, unroll=8)

    for tile in range(tiles):
        goals = jnp.concatenate([goal_ref[tile], jnp.zeros((5, TILE), f32)], axis=0).T
        for channel in range(3):
            high, low = halves(color_ref[tile, channel], 2)
            color = jnp.dot(
                jnp.concatenate([high, low], axis=1), ones, preferred_element_type=f32
            )
            error = color - goals[:, channel : channel + 1]
            slope_ref[tile, channel] = error * lax.rsqrt(error * error + SMOOTHING) * (1.0 / 3.0)
    carry_ref[...] = jnp.zeros_like(carry_ref)

    def total(values):
        return jnp.sum(values, axis=0, keepdims=True)

    def backward(step, carry):
        layer = LIST - 1 - step
        color_grads = []
        for tile in range(tiles):
            slot = jnp.maximum(entry_of(tile, layer), 0)
            shades = [wide(feature(slot, 6 + channel)) for channel in range(3)]
            grads = [jnp.zeros((half, BLOCK), f32) for _ in range(3)]
            for row in range(SIDE):
                parts = []
                for part in range(2):
                    where = row_of(row, part)
                    weight = weight_ref[tile, layer, where]
                    pulled = [weight * slope_ref[tile, channel, where] for channel in range(3)]
                    grads = [grads[channel] + pulled[channel] for channel in range(3)]
                    gain = pulled[0] * shades[0] + pulled[1] * shades[1] + pulled[2] * shades[2]
                    weight_ref[tile, layer, where] = gain
                    parts.append(gain)
                split_row(tile, row, parts)
            color_grads.append([total(grad) for grad in grads])
        sums = add_up(later)
        for tile in range(tiles):
            slot = jnp.maximum(entry_of(tile, layer), 0)
            delta_x, place_y = offsets(tile, slot)
            flat = [jnp.zeros((half, BLOCK), f32) for _ in range(2)]
            tilt = [jnp.zeros((half, BLOCK), f32) for _ in range(2)]
            bend = jnp.zeros((half, BLOCK), f32)
            for row in range(SIDE):
                delta_y = (row - (SIDE / 2 - 0.5)) - place_y
                for part in range(2):
                    where = row_of(row, part)
                    start = tile * TILE + where.start
                    alpha = alpha_ref[tile, layer, where]
                    after = carry_ref[tile, where]
                    behind = sums[start : start + half, :BLOCK] + after
                    carry_ref[tile, where] = after + sums[start : start + half, BLOCK:]
                    power_grad = weight_ref[tile, layer, where] - behind * (alpha / (1.0 - alpha))
                    turned = power_grad * delta_y
                    flat[part] += power_grad
                    tilt[part] += turned
                    bend += turned * delta_y
            leaned = [flat[part] * delta_x[part] for part in range(2)]
            sum_x = total(leaned[0] + leaned[1])
            sum_y = total(tilt[0] + tilt[1])
            conic_a, conic_b, conic_c = feature(slot, 2), feature(slot, 3), feature(slot, 4)
            results = [
                conic_a * sum_x + conic_b * sum_y,
                conic_b * sum_x + conic_c * sum_y,
                -0.5 * total(leaned[0] * delta_x[0] + leaned[1] * delta_x[1]),
                -total(tilt[0] * delta_x[0] + tilt[1] * delta_x[1]),
                -0.5 * total(bend),
                total(flat[0] + flat[1]),
            ] + color_grads[tile]
            for index in range(FEATS):
                out_ref[pl.ds(slot * FEATS + index, 1)] += results[index]
        return carry

    lax.fori_loop(0, LIST, backward, 0, unroll=8)


def collect_kernel(keys_ref, slots_ref, out_ref):
    copies, count = out_ref.shape[:2]
    width = slots_ref.shape[0]
    wanted = lax.broadcasted_iota(jnp.int32, (count, width), 0)
    picker = jnp.where(keys_ref[...] == wanted, 1.0, 0.0).astype(jnp.bfloat16)
    total = jnp.zeros((count, BLOCK), jnp.float32)
    for piece in halves(slots_ref[...], 3):
        total += jnp.dot(picker, piece, preferred_element_type=jnp.float32)
    for copy in range(copies):
        out_ref[copy] = total


def update_kernel(
    blocks_here,
    center_x,
    center_y,
    cot_ref,
    params_ref,
    adam_m_ref,
    adam_v_ref,
    new_params_ref,
    new_m_ref,
    new_v_ref,
    grad_ref,
):
    codes = 2 * blocks_here
    rows = code_rows(params_ref, blocks_here)
    shift = code_shift(blocks_here)
    summed = cot_ref[0]
    for group in range(1, cot_ref.shape[0]):
        summed = summed + cot_ref[group]
    cots = [summed[codes * feat : codes * (feat + 1)] for feat in range(FEATS)]
    used = rows[:10] + rows[11:]

    def shown_of(values):
        return project(values[:10] + [None] + values[10:], shift, center_x, center_y)

    _, pull = jax.vjp(shown_of, used)
    grads = pull(cots[:5] + cots[6:])[0]
    logit_grad = cots[5] * (1.0 - jax.nn.sigmoid(rows[10]))
    grads = grads[:10] + [logit_grad] + grads[10:]
    for row in range(PARAMS):
        both = grads[row][:blocks_here] + grads[row][blocks_here:]
        for block in range(blocks_here):
            grad_ref[row : row + 1, block * BLOCK : (block + 1) * BLOCK] = both[block : block + 1]
    grad = grad_ref[...]
    new_m = BETA_ONE * adam_m_ref[...] + (1.0 - BETA_ONE) * grad
    new_v = BETA_TWO * adam_v_ref[...] + (1.0 - BETA_TWO) * grad * grad
    m_hat = new_m * (1.0 / (1.0 - BETA_ONE**ADAM_STEP))
    v_hat = new_v * (1.0 / (1.0 - BETA_TWO**ADAM_STEP))
    row = lax.broadcasted_iota(jnp.int32, grad.shape, 0)
    rates = jnp.full(grad.shape, RATES[0][1], jnp.float32)
    for first, rate in RATES[1:]:
        rates = jnp.where(row >= first, jnp.float32(rate), rates)
    new_params_ref[...] = params_ref[...] - rates * m_hat / (jnp.sqrt(v_hat) + ADAM_EPS)
    new_m_ref[...] = new_m
    new_v_ref[...] = new_v


def vmem(count):
    return [pl.BlockSpec(memory_space=VMEM)] * count


def smem(count):
    return [pl.BlockSpec(memory_space=SMEM)] * count


def run_project(params, provided, center_x, center_y, limit):
    blocks_here = params.shape[1] // BLOCK
    codes = 2 * blocks_here
    f32 = jnp.float32
    return pl.pallas_call(
        lambda *refs: project_kernel(blocks_here, center_x, center_y, *refs),
        out_shape=jax.ShapeDtypeStruct((provided.shape[0] * FEATS, BLOCK), f32),
        in_specs=[pl.BlockSpec(memory_space=pltpu.MemorySpace.HBM)] * 2,
        out_specs=vmem(1)[0],
        scratch_shapes=[
            pltpu.SMEM(provided.shape, jnp.int32),
            pltpu.VMEM(params.shape, f32),
            pltpu.VMEM((codes, FEATS, BLOCK), f32),
            pltpu.SemaphoreType.DMA((2,)),
        ],
        compiler_params=pltpu.CompilerParams(vmem_limit_bytes=WHOLE_VMEM),
        name="project",
    )(provided, params)


def run_render(scalars, incoming, goals, tiles_y, limit):
    tiles = goals.shape[0]
    f32 = jnp.float32
    pairs = pltpu.VMEM((tiles, LIST, TILE, BLOCK), f32)
    return pl.pallas_call(
        lambda *refs: render_kernel(tiles_y, *refs),
        out_shape=jax.ShapeDtypeStruct(incoming.shape, f32),
        in_specs=smem(1) + vmem(2),
        out_specs=vmem(1)[0],
        scratch_shapes=[
            pairs,
            pairs,
            pltpu.VMEM((tiles * TILE, 2 * BLOCK), jnp.bfloat16),
            pltpu.VMEM((tiles, TILE, BLOCK), f32),
            pltpu.VMEM((tiles, 3, TILE, BLOCK), f32),
            pltpu.VMEM((tiles, 3, TILE, BLOCK), f32),
        ],
        compiler_params=limit,
        name="render",
    )(scalars, incoming, goals)


def run_collect(keys, returned, codes, groups, limit):
    return pl.pallas_call(
        collect_kernel,
        out_shape=jax.ShapeDtypeStruct((groups, FEATS * codes, BLOCK), jnp.float32),
        in_specs=vmem(2),
        out_specs=vmem(1)[0],
        compiler_params=limit,
        name="collect",
    )(keys, returned)


def run_update(gathered, params, adam_m, adam_v, center_x, center_y, limit):
    blocks_here = params.shape[1] // BLOCK
    shape = jax.ShapeDtypeStruct(params.shape, jnp.float32)
    return pl.pallas_call(
        lambda *refs: update_kernel(blocks_here, center_x, center_y, *refs),
        out_shape=(shape,) * 4,
        in_specs=vmem(4),
        out_specs=tuple(vmem(4)),
        compiler_params=limit,
        name="update",
    )(gathered, params, adam_m, adam_v)


def exchange(slots, dev_count):
    sent = slots.reshape(dev_count, 1, SLOT)
    return lax.all_to_all(sent, "dev", split_axis=0, concat_axis=0, tiled=True).reshape(slots.shape)


def on_device(params, adam_m, adam_v, target, tile_ids, send_blocks, tile_lists):
    dev_count = lax.axis_size("dev")
    blocks_here = params.shape[1] // BLOCK
    codes = 2 * blocks_here
    tiles_y = dev_count * blocks_here // TILES_X
    center_x = 8.0 * TILES_X
    center_y = 8.0 * tiles_y
    limit = pltpu.CompilerParams(vmem_limit_bytes=VMEM_LIMIT)
    provided = send_blocks.reshape(-1)
    scalars = jnp.concatenate([tile_ids.reshape(-1), tile_lists.reshape(-1)])

    outgoing = run_project(params, provided, center_x, center_y, limit)
    incoming = exchange(outgoing, dev_count)
    goals = target.reshape(target.shape[2:])
    cotangent = run_render(scalars, incoming, goals, tiles_y, limit)
    returned = exchange(cotangent, dev_count)
    order = jnp.arange(FEATS, dtype=jnp.int32) * codes
    keys = jnp.where(provided[:, None] >= 0, provided[:, None] + order[None, :], -1)
    groups = lax.axis_size("rep")
    keys = keys.reshape(1, dev_count * FEATS)
    per_code = run_collect(keys, returned, codes, groups, limit)
    gathered = lax.all_to_all(per_code, "rep", split_axis=0, concat_axis=0, tiled=True)
    return run_update(gathered, params, adam_m, adam_v, center_x, center_y, limit)


def solution(mesh):
    placed = (
        P(None, "dev"),
        P(None, "dev"),
        P(None, "dev"),
        P("rep", "dev", None, None, None),
        P("rep", "dev", None),
        P("rep", "dev", None, None),
        P("rep", "dev", None, None),
    )
    return jax.shard_map(
        on_device,
        mesh=mesh,
        in_specs=placed,
        out_specs=(P(None, "dev"), P(None, "dev"), P(None, "dev"), P(None, "dev")),
        check_vma=False,
    )
```

```python
import jax
import jax.numpy as jnp
from jax import lax
from jax.experimental import pallas as pl
from jax.experimental.pallas import tpu as pltpu
from jax.sharding import PartitionSpec as P

BLOCK = 128
PARAMS = 59
FEATS = 9
SLOT = FEATS * BLOCK
TILE = 256
SIDE = 16
LIST = 8
OUT_PARTS = 4
TILES_X = 64
ADAM_STEP = 1000

FOCAL = 1100.0
DEPTH_ZERO = 20.0
BASELINE = 16.0 * DEPTH_ZERO / FOCAL
BLUR = 0.3
SMOOTHING = 0.0001
BETA_ONE = 0.9
BETA_TWO = 0.999
ADAM_EPS = 1e-15
SH_ZERO = 0.28209479177387814
SH_ONE = 0.4886025119029199
SH_TWO = [
    1.0925484305920792,
    -1.0925484305920792,
    0.31539156525252005,
    -1.0925484305920792,
    0.5462742152960396,
]
SH_THREE = [
    -0.5900435899266435,
    2.890611442640554,
    -0.4570457994644658,
    0.3731763325901154,
    -0.4570457994644658,
    1.445305721320277,
    -0.5900435899266435,
]
RATES = [(0, 0.00016), (3, 0.005), (6, 0.001), (10, 0.05), (11, 0.0025), (14, 0.000125)]

VMEM_LIMIT = 40 * 1024 * 1024
WHOLE_VMEM = 60 * 1024 * 1024
SMEM = pltpu.MemorySpace.SMEM
VMEM = pltpu.MemorySpace.VMEM


def sh_basis(unit_x, unit_y, unit_z):
    square_x = unit_x * unit_x
    square_y = unit_y * unit_y
    square_z = unit_z * unit_z
    return [
        SH_ZERO + 0.0 * unit_x,
        -SH_ONE * unit_y,
        SH_ONE * unit_z,
        -SH_ONE * unit_x,
        SH_TWO[0] * unit_x * unit_y,
        SH_TWO[1] * unit_y * unit_z,
        SH_TWO[2] * (2.0 * square_z - square_x - square_y),
        SH_TWO[3] * unit_x * unit_z,
        SH_TWO[4] * (square_x - square_y),
        SH_THREE[0] * unit_y * (3.0 * square_x - square_y),
        SH_THREE[1] * unit_x * unit_y * unit_z,
        SH_THREE[2] * unit_y * (4.0 * square_z - square_x - square_y),
        SH_THREE[3] * unit_z * (2.0 * square_z - 3.0 * square_x - 3.0 * square_y),
        SH_THREE[4] * unit_x * (4.0 * square_z - square_x - square_y),
        SH_THREE[5] * unit_z * (square_x - square_y),
        SH_THREE[6] * unit_x * (square_x - 3.0 * square_y),
    ]


def project(rows, shift, center_x, center_y):
    offset_x = rows[0] - shift
    offset_y = rows[1]
    depth = rows[2]
    inverse = 1.0 / depth
    focal_depth = FOCAL * inverse
    screen_x = focal_depth * offset_x + center_x
    screen_y = focal_depth * offset_y + center_y
    scales = [jnp.exp(rows[3 + index]) for index in range(3)]
    norm = jnp.sqrt(
        rows[6] * rows[6] + rows[7] * rows[7] + rows[8] * rows[8] + rows[9] * rows[9]
    )
    quat_w, quat_x, quat_y, quat_z = [rows[6 + index] / norm for index in range(4)]
    rotation = [
        [
            1.0 - 2.0 * (quat_y * quat_y + quat_z * quat_z),
            2.0 * (quat_x * quat_y - quat_w * quat_z),
            2.0 * (quat_x * quat_z + quat_w * quat_y),
        ],
        [
            2.0 * (quat_x * quat_y + quat_w * quat_z),
            1.0 - 2.0 * (quat_x * quat_x + quat_z * quat_z),
            2.0 * (quat_y * quat_z - quat_w * quat_x),
        ],
        [
            2.0 * (quat_x * quat_z - quat_w * quat_y),
            2.0 * (quat_y * quat_z + quat_w * quat_x),
            1.0 - 2.0 * (quat_x * quat_x + quat_y * quat_y),
        ],
    ]
    slope_x = focal_depth * offset_x * inverse
    slope_y = focal_depth * offset_y * inverse
    first_row = [
        (focal_depth * rotation[0][index] - slope_x * rotation[2][index]) * scales[index]
        for index in range(3)
    ]
    second_row = [
        (focal_depth * rotation[1][index] - slope_y * rotation[2][index]) * scales[index]
        for index in range(3)
    ]
    sigma_xx = (
        first_row[0] * first_row[0]
        + first_row[1] * first_row[1]
        + first_row[2] * first_row[2]
        + BLUR
    )
    sigma_xy = (
        first_row[0] * second_row[0] + first_row[1] * second_row[1] + first_row[2] * second_row[2]
    )
    sigma_yy = (
        second_row[0] * second_row[0]
        + second_row[1] * second_row[1]
        + second_row[2] * second_row[2]
        + BLUR
    )
    determinant = sigma_xx * sigma_yy - sigma_xy * sigma_xy
    distance = jnp.sqrt(offset_x * offset_x + offset_y * offset_y + depth * depth)
    basis = sh_basis(offset_x / distance, offset_y / distance, depth / distance)
    colors = []
    for channel in range(3):
        total = basis[0] * rows[11 + channel]
        for index in range(1, 16):
            total = total + basis[index] * rows[11 + 3 * index + channel]
        colors.append(jnp.maximum(total + 0.5, 0.0))
    return [
        screen_x,
        screen_y,
        sigma_yy / determinant,
        -sigma_xy / determinant,
        sigma_xx / determinant,
        colors[0],
        colors[1],
        colors[2],
    ]


def code_rows(params_ref, blocks_here):
    rows = []
    for row in range(PARAMS):
        parts = [
            params_ref[row : row + 1, block * BLOCK : (block + 1) * BLOCK]
            for block in range(blocks_here)
        ]
        rows.append(jnp.concatenate(parts + parts, axis=0))
    return rows


def code_shift(blocks_here):
    code = lax.broadcasted_iota(jnp.int32, (2 * blocks_here, BLOCK), 0)
    return jnp.where(code >= blocks_here, BASELINE, 0.0).astype(jnp.float32)


def halves(values, pieces):
    out = []
    rest = values
    for index in range(pieces):
        part = rest.astype(jnp.bfloat16)
        out.append(part)
        if index < pieces - 1:
            rest = rest - part.astype(jnp.float32)
    return out


def project_kernel(
    blocks_here,
    center_x,
    center_y,
    codes_hbm,
    params_hbm,
    out_hbm,
    codes_ref,
    params_ref,
    table_ref,
    out_ref,
    sems,
    out_sems,
):
    copies = [pltpu.make_async_copy(codes_hbm, codes_ref, sems.at[blocks_here])]
    for block in range(blocks_here):
        where = (slice(None), pl.ds(block * BLOCK, BLOCK))
        copies.append(
            pltpu.make_async_copy(params_hbm.at[where], params_ref.at[where], sems.at[block])
        )
    for copy in copies:
        copy.start()
    for copy in copies[1:]:
        copy.wait()
    rows = code_rows(params_ref, blocks_here)
    shown = project(rows, code_shift(blocks_here), center_x, center_y)
    shown = shown[:5] + [jax.nn.sigmoid(rows[10])] + shown[5:]
    for code in range(2 * blocks_here):
        for feat in range(FEATS):
            table_ref[code, feat : feat + 1] = shown[feat][code : code + 1]
    copies[0].wait()

    def fill(target, carry):
        code = jnp.maximum(codes_ref[target], 0)
        out_ref[pl.ds(target * FEATS, 8)] = table_ref[code, 0:8]
        out_ref[pl.ds(target * FEATS + 8, 1)] = table_ref[code, 8:9]
        return carry

    rows = out_ref.shape[0] // OUT_PARTS
    parts = []
    for index in range(OUT_PARTS):
        first = index * (rows // FEATS)
        lax.fori_loop(first, first + rows // FEATS, fill, 0, unroll=32)
        where = pl.ds(index * rows, rows)
        parts.append(
            pltpu.make_async_copy(out_ref.at[where], out_hbm.at[where], out_sems.at[index])
        )
        parts[-1].start()
    for part in parts:
        part.wait()


def render_kernel(
    tiles_y,
    scalars_ref,
    slots_ref,
    goal_ref,
    out_ref,
    alpha_ref,
    weight_ref,
    pieces_ref,
    carry_ref,
    color_ref,
    slope_ref,
):
    tiles = goal_ref.shape[0]
    per_view = TILES_X * tiles_y
    f32 = jnp.float32
    half = SIDE // 2
    lane = lax.broadcasted_iota(jnp.int32, (2 * BLOCK, 2 * BLOCK), 1)
    depth = lax.broadcasted_iota(jnp.int32, (2 * BLOCK, 2 * BLOCK), 0) % BLOCK
    earlier = jnp.where((lane >= BLOCK) | (depth < lane), 1.0, 0.0).astype(jnp.bfloat16)
    later = jnp.where((lane >= BLOCK) | (depth > lane), 1.0, 0.0).astype(jnp.bfloat16)
    ones = jnp.ones((2 * BLOCK, BLOCK), jnp.bfloat16)
    column = lax.broadcasted_iota(jnp.int32, (half, BLOCK), 0).astype(f32) - (SIDE / 2 - 0.5)

    out_ref[...] = jnp.zeros_like(out_ref)

    def entry_of(tile, layer):
        return scalars_ref[tiles + tile * LIST + layer]

    def feature(slot, index):
        return slots_ref[pl.ds(slot * FEATS + index, 1)]

    def wide(row):
        return jnp.broadcast_to(row, (half, BLOCK))

    def center(tile):
        within = lax.rem(scalars_ref[tile], per_view)
        middle_x = (lax.rem(within, TILES_X) * SIDE + half).astype(f32)
        middle_y = (lax.div(within, TILES_X) * SIDE + half).astype(f32)
        return middle_x, middle_y

    def row_of(index, part):
        start = index * SIDE + part * half
        return slice(start, start + half)

    def offsets(tile, slot):
        middle_x, middle_y = center(tile)
        place_x = wide(feature(slot, 0) - middle_x)
        place_y = wide(feature(slot, 1) - middle_y)
        return [column + part * half - place_x for part in range(2)], place_y

    def split_row(tile, row, parts):
        pairs = [halves(part, 2) for part in parts]
        start = tile * TILE + row * SIDE
        for side in range(2):
            both = jnp.concatenate([pair[side] for pair in pairs], axis=0)
            pieces_ref[start : start + SIDE, side * BLOCK : (side + 1) * BLOCK] = both

    def add_up(matrix):
        return jnp.concatenate(
            [
                jnp.dot(
                    pieces_ref[tile * TILE : (tile + 1) * TILE],
                    matrix,
                    preferred_element_type=f32,
                )
                for tile in range(tiles)
            ],
            axis=0,
        )

    def forward(layer, carry):
        for tile in range(tiles):
            entry = entry_of(tile, layer)
            slot = jnp.maximum(entry, 0)
            live = jnp.where(entry >= 0, 1.0, 0.0).astype(f32)
            delta_x, place_y = offsets(tile, slot)
            half_x = [wide(-0.5 * feature(slot, 2)) * delta * delta for delta in delta_x]
            cross = [wide(-feature(slot, 3)) * delta for delta in delta_x]
            half_y = wide(-0.5 * feature(slot, 4))
            opacity = wide(feature(slot, 5) * live)
            for row in range(SIDE):
                delta_y = (row - (SIDE / 2 - 0.5)) - place_y
                scaled_y = half_y * delta_y
                logs = []
                for part in range(2):
                    power = half_x[part] + delta_y * (cross[part] + scaled_y)
                    alpha = opacity * jnp.exp(power)
                    alpha_ref[tile, layer, row_of(row, part)] = alpha
                    logs.append(jnp.log(1.0 - alpha))
                split_row(tile, row, logs)
        sums = add_up(earlier)
        for tile in range(tiles):
            slot = jnp.maximum(entry_of(tile, layer), 0)
            shades = [wide(feature(slot, 6 + channel)) for channel in range(3)]
            for row in range(SIDE):
                for part in range(2):
                    where = row_of(row, part)
                    start = tile * TILE + where.start
                    before = carry_ref[tile, where]
                    weight = alpha_ref[tile, layer, where] * jnp.exp(
                        sums[start : start + half, :BLOCK] + before
                    )
                    weight_ref[tile, layer, where] = weight
                    carry_ref[tile, where] = before + sums[start : start + half, BLOCK:]
                    for channel in range(3):
                        color_ref[tile, channel, where] += weight * shades[channel]
        return carry

    color_ref[...] = jnp.zeros_like(color_ref)
    carry_ref[...] = jnp.zeros_like(carry_ref)
    lax.fori_loop(0, LIST, forward, 0, unroll=8)

    for tile in range(tiles):
        goals = jnp.concatenate([goal_ref[tile], jnp.zeros((5, TILE), f32)], axis=0).T
        for channel in range(3):
            high, low = halves(color_ref[tile, channel], 2)
            color = jnp.dot(
                jnp.concatenate([high, low], axis=1), ones, preferred_element_type=f32
            )
            error = color - goals[:, channel : channel + 1]
            slope_ref[tile, channel] = error * lax.rsqrt(error * error + SMOOTHING) * (1.0 / 3.0)
    carry_ref[...] = jnp.zeros_like(carry_ref)

    def total(values):
        return jnp.sum(values, axis=0, keepdims=True)

    def backward(step, carry):
        layer = LIST - 1 - step
        color_grads = []
        for tile in range(tiles):
            slot = jnp.maximum(entry_of(tile, layer), 0)
            shades = [wide(feature(slot, 6 + channel)) for channel in range(3)]
            grads = [jnp.zeros((half, BLOCK), f32) for _ in range(3)]
            for row in range(SIDE):
                parts = []
                for part in range(2):
                    where = row_of(row, part)
                    weight = weight_ref[tile, layer, where]
                    pulled = [weight * slope_ref[tile, channel, where] for channel in range(3)]
                    grads = [grads[channel] + pulled[channel] for channel in range(3)]
                    gain = pulled[0] * shades[0] + pulled[1] * shades[1] + pulled[2] * shades[2]
                    weight_ref[tile, layer, where] = gain
                    parts.append(gain)
                split_row(tile, row, parts)
            color_grads.append([total(grad) for grad in grads])
        sums = add_up(later)
        for tile in range(tiles):
            slot = jnp.maximum(entry_of(tile, layer), 0)
            delta_x, place_y = offsets(tile, slot)
            flat = [jnp.zeros((half, BLOCK), f32) for _ in range(2)]
            tilt = [jnp.zeros((half, BLOCK), f32) for _ in range(2)]
            bend = jnp.zeros((half, BLOCK), f32)
            for row in range(SIDE):
                delta_y = (row - (SIDE / 2 - 0.5)) - place_y
                for part in range(2):
                    where = row_of(row, part)
                    start = tile * TILE + where.start
                    alpha = alpha_ref[tile, layer, where]
                    after = carry_ref[tile, where]
                    behind = sums[start : start + half, :BLOCK] + after
                    carry_ref[tile, where] = after + sums[start : start + half, BLOCK:]
                    power_grad = weight_ref[tile, layer, where] - behind * (alpha / (1.0 - alpha))
                    turned = power_grad * delta_y
                    flat[part] += power_grad
                    tilt[part] += turned
                    bend += turned * delta_y
            leaned = [flat[part] * delta_x[part] for part in range(2)]
            sum_x = total(leaned[0] + leaned[1])
            sum_y = total(tilt[0] + tilt[1])
            conic_a, conic_b, conic_c = feature(slot, 2), feature(slot, 3), feature(slot, 4)
            results = [
                conic_a * sum_x + conic_b * sum_y,
                conic_b * sum_x + conic_c * sum_y,
                -0.5 * total(leaned[0] * delta_x[0] + leaned[1] * delta_x[1]),
                -total(tilt[0] * delta_x[0] + tilt[1] * delta_x[1]),
                -0.5 * total(bend),
                total(flat[0] + flat[1]),
            ] + color_grads[tile]
            for index in range(FEATS):
                out_ref[pl.ds(slot * FEATS + index, 1)] += results[index]
        return carry

    lax.fori_loop(0, LIST, backward, 0, unroll=8)


def collect_kernel(keys_ref, slots_ref, out_ref):
    copies, count = out_ref.shape[:2]
    width = slots_ref.shape[0]
    wanted = lax.broadcasted_iota(jnp.int32, (count, width), 0)
    picker = jnp.where(keys_ref[...] == wanted, 1.0, 0.0).astype(jnp.bfloat16)
    total = jnp.zeros((count, BLOCK), jnp.float32)
    for piece in halves(slots_ref[...], 3):
        total += jnp.dot(picker, piece, preferred_element_type=jnp.float32)
    for copy in range(copies):
        out_ref[copy] = total


def update_kernel(
    blocks_here,
    center_x,
    center_y,
    cot_ref,
    params_ref,
    adam_m_ref,
    adam_v_ref,
    new_params_ref,
    new_m_ref,
    new_v_ref,
    grad_ref,
):
    codes = 2 * blocks_here
    rows = code_rows(params_ref, blocks_here)
    shift = code_shift(blocks_here)
    summed = cot_ref[0]
    for group in range(1, cot_ref.shape[0]):
        summed = summed + cot_ref[group]
    cots = [summed[codes * feat : codes * (feat + 1)] for feat in range(FEATS)]
    used = rows[:10] + rows[11:]

    def shown_of(values):
        return project(values[:10] + [None] + values[10:], shift, center_x, center_y)

    _, pull = jax.vjp(shown_of, used)
    grads = pull(cots[:5] + cots[6:])[0]
    logit_grad = cots[5] * (1.0 - jax.nn.sigmoid(rows[10]))
    grads = grads[:10] + [logit_grad] + grads[10:]
    for row in range(PARAMS):
        both = grads[row][:blocks_here] + grads[row][blocks_here:]
        for block in range(blocks_here):
            grad_ref[row : row + 1, block * BLOCK : (block + 1) * BLOCK] = both[block : block + 1]
    grad = grad_ref[...]
    new_m = BETA_ONE * adam_m_ref[...] + (1.0 - BETA_ONE) * grad
    new_v = BETA_TWO * adam_v_ref[...] + (1.0 - BETA_TWO) * grad * grad
    m_hat = new_m * (1.0 / (1.0 - BETA_ONE**ADAM_STEP))
    v_hat = new_v * (1.0 / (1.0 - BETA_TWO**ADAM_STEP))
    row = lax.broadcasted_iota(jnp.int32, grad.shape, 0)
    rates = jnp.full(grad.shape, RATES[0][1], jnp.float32)
    for first, rate in RATES[1:]:
        rates = jnp.where(row >= first, jnp.float32(rate), rates)
    new_params_ref[...] = params_ref[...] - rates * m_hat / (jnp.sqrt(v_hat) + ADAM_EPS)
    new_m_ref[...] = new_m
    new_v_ref[...] = new_v


def vmem(count):
    return [pl.BlockSpec(memory_space=VMEM)] * count


def smem(count):
    return [pl.BlockSpec(memory_space=SMEM)] * count


def run_project(params, provided, center_x, center_y, limit):
    blocks_here = params.shape[1] // BLOCK
    codes = 2 * blocks_here
    f32 = jnp.float32
    return pl.pallas_call(
        lambda *refs: project_kernel(blocks_here, center_x, center_y, *refs),
        out_shape=jax.ShapeDtypeStruct((provided.shape[0] * FEATS, BLOCK), f32),
        in_specs=[pl.BlockSpec(memory_space=pltpu.MemorySpace.HBM)] * 2,
        out_specs=pl.BlockSpec(memory_space=pl.ANY),
        scratch_shapes=[
            pltpu.SMEM(provided.shape, jnp.int32),
            pltpu.VMEM(params.shape, f32),
            pltpu.VMEM((codes, FEATS, BLOCK), f32),
            pltpu.VMEM((provided.shape[0] * FEATS, BLOCK), f32),
            pltpu.SemaphoreType.DMA((blocks_here + 1,)),
            pltpu.SemaphoreType.DMA((OUT_PARTS,)),
        ],
        compiler_params=pltpu.CompilerParams(vmem_limit_bytes=WHOLE_VMEM),
        name="project",
    )(provided, params)


def run_render(scalars, incoming, goals, tiles_y, limit):
    tiles = goals.shape[0]
    f32 = jnp.float32
    pairs = pltpu.VMEM((tiles, LIST, TILE, BLOCK), f32)
    return pl.pallas_call(
        lambda *refs: render_kernel(tiles_y, *refs),
        out_shape=jax.ShapeDtypeStruct(incoming.shape, f32),
        in_specs=smem(1) + vmem(2),
        out_specs=vmem(1)[0],
        scratch_shapes=[
            pairs,
            pairs,
            pltpu.VMEM((tiles * TILE, 2 * BLOCK), jnp.bfloat16),
            pltpu.VMEM((tiles, TILE, BLOCK), f32),
            pltpu.VMEM((tiles, 3, TILE, BLOCK), f32),
            pltpu.VMEM((tiles, 3, TILE, BLOCK), f32),
        ],
        compiler_params=limit,
        name="render",
    )(scalars, incoming, goals)


def run_collect(keys, returned, codes, groups, limit):
    return pl.pallas_call(
        collect_kernel,
        out_shape=jax.ShapeDtypeStruct((groups, FEATS * codes, BLOCK), jnp.float32),
        in_specs=vmem(2),
        out_specs=vmem(1)[0],
        compiler_params=limit,
        name="collect",
    )(keys, returned)


def run_update(gathered, params, adam_m, adam_v, center_x, center_y, limit):
    blocks_here = params.shape[1] // BLOCK
    shape = jax.ShapeDtypeStruct(params.shape, jnp.float32)
    return pl.pallas_call(
        lambda *refs: update_kernel(blocks_here, center_x, center_y, *refs),
        out_shape=(shape,) * 4,
        in_specs=vmem(4),
        out_specs=tuple(vmem(4)),
        compiler_params=limit,
        name="update",
    )(gathered, params, adam_m, adam_v)


def exchange(slots, dev_count):
    sent = slots.reshape(dev_count, 1, SLOT)
    return lax.all_to_all(sent, "dev", split_axis=0, concat_axis=0, tiled=True).reshape(slots.shape)


def on_device(params, adam_m, adam_v, target, tile_ids, send_blocks, tile_lists):
    dev_count = lax.axis_size("dev")
    blocks_here = params.shape[1] // BLOCK
    codes = 2 * blocks_here
    tiles_y = dev_count * blocks_here // TILES_X
    center_x = 8.0 * TILES_X
    center_y = 8.0 * tiles_y
    limit = pltpu.CompilerParams(vmem_limit_bytes=VMEM_LIMIT)
    provided = send_blocks.reshape(-1)
    scalars = jnp.concatenate([tile_ids.reshape(-1), tile_lists.reshape(-1)])
    order = jnp.arange(FEATS, dtype=jnp.int32) * codes
    keys = jnp.where(provided[:, None] >= 0, provided[:, None] + order[None, :], -1)
    keys = keys.reshape(1, dev_count * FEATS)
    scalars, keys = lax.optimization_barrier((scalars, keys))

    outgoing = run_project(params, provided, center_x, center_y, limit)
    incoming = exchange(outgoing, dev_count)
    goals = target.reshape(target.shape[2:])
    cotangent = run_render(scalars, incoming, goals, tiles_y, limit)
    returned = exchange(cotangent, dev_count)
    groups = lax.axis_size("rep")
    per_code = run_collect(keys, returned, codes, groups, limit)
    gathered = lax.all_to_all(per_code, "rep", split_axis=0, concat_axis=0, tiled=True)
    return run_update(gathered, params, adam_m, adam_v, center_x, center_y, limit)


def solution(mesh):
    placed = (
        P(None, "dev"),
        P(None, "dev"),
        P(None, "dev"),
        P("rep", "dev", None, None, None),
        P("rep", "dev", None),
        P("rep", "dev", None, None),
        P("rep", "dev", None, None),
    )
    return jax.shard_map(
        on_device,
        mesh=mesh,
        in_specs=placed,
        out_specs=(P(None, "dev"), P(None, "dev"), P(None, "dev"), P(None, "dev")),
        check_vma=False,
    )
```

```python
import jax
import jax.numpy as jnp
from jax import lax
from jax.experimental import pallas as pl
from jax.experimental.pallas import tpu as pltpu
from jax.sharding import PartitionSpec as P

BLOCK = 128
PARAMS = 59
FEATS = 9
SLOT = FEATS * BLOCK
TILE = 256
SIDE = 16
LIST = 8
LOG2_E = 1.4426950408889634
OUT_PARTS = 4
TILES_X = 64
ADAM_STEP = 1000

FOCAL = 1100.0
DEPTH_ZERO = 20.0
BASELINE = 16.0 * DEPTH_ZERO / FOCAL
BLUR = 0.3
SMOOTHING = 0.0001
BETA_ONE = 0.9
BETA_TWO = 0.999
ADAM_EPS = 1e-15
SH_ZERO = 0.28209479177387814
SH_ONE = 0.4886025119029199
SH_TWO = [
    1.0925484305920792,
    -1.0925484305920792,
    0.31539156525252005,
    -1.0925484305920792,
    0.5462742152960396,
]
SH_THREE = [
    -0.5900435899266435,
    2.890611442640554,
    -0.4570457994644658,
    0.3731763325901154,
    -0.4570457994644658,
    1.445305721320277,
    -0.5900435899266435,
]
RATES = [(0, 0.00016), (3, 0.005), (6, 0.001), (10, 0.05), (11, 0.0025), (14, 0.000125)]

VMEM_LIMIT = 40 * 1024 * 1024
WHOLE_VMEM = 60 * 1024 * 1024
SMEM = pltpu.MemorySpace.SMEM
VMEM = pltpu.MemorySpace.VMEM


def sh_basis(unit_x, unit_y, unit_z):
    square_x = unit_x * unit_x
    square_y = unit_y * unit_y
    square_z = unit_z * unit_z
    return [
        SH_ZERO + 0.0 * unit_x,
        -SH_ONE * unit_y,
        SH_ONE * unit_z,
        -SH_ONE * unit_x,
        SH_TWO[0] * unit_x * unit_y,
        SH_TWO[1] * unit_y * unit_z,
        SH_TWO[2] * (2.0 * square_z - square_x - square_y),
        SH_TWO[3] * unit_x * unit_z,
        SH_TWO[4] * (square_x - square_y),
        SH_THREE[0] * unit_y * (3.0 * square_x - square_y),
        SH_THREE[1] * unit_x * unit_y * unit_z,
        SH_THREE[2] * unit_y * (4.0 * square_z - square_x - square_y),
        SH_THREE[3] * unit_z * (2.0 * square_z - 3.0 * square_x - 3.0 * square_y),
        SH_THREE[4] * unit_x * (4.0 * square_z - square_x - square_y),
        SH_THREE[5] * unit_z * (square_x - square_y),
        SH_THREE[6] * unit_x * (square_x - 3.0 * square_y),
    ]


def project(rows, shift, center_x, center_y):
    offset_x = rows[0] - shift
    offset_y = rows[1]
    depth = rows[2]
    inverse = 1.0 / depth
    focal_depth = FOCAL * inverse
    screen_x = focal_depth * offset_x + center_x
    screen_y = focal_depth * offset_y + center_y
    scales = [jnp.exp(rows[3 + index]) for index in range(3)]
    norm = jnp.sqrt(
        rows[6] * rows[6] + rows[7] * rows[7] + rows[8] * rows[8] + rows[9] * rows[9]
    )
    quat_w, quat_x, quat_y, quat_z = [rows[6 + index] / norm for index in range(4)]
    rotation = [
        [
            1.0 - 2.0 * (quat_y * quat_y + quat_z * quat_z),
            2.0 * (quat_x * quat_y - quat_w * quat_z),
            2.0 * (quat_x * quat_z + quat_w * quat_y),
        ],
        [
            2.0 * (quat_x * quat_y + quat_w * quat_z),
            1.0 - 2.0 * (quat_x * quat_x + quat_z * quat_z),
            2.0 * (quat_y * quat_z - quat_w * quat_x),
        ],
        [
            2.0 * (quat_x * quat_z - quat_w * quat_y),
            2.0 * (quat_y * quat_z + quat_w * quat_x),
            1.0 - 2.0 * (quat_x * quat_x + quat_y * quat_y),
        ],
    ]
    slope_x = focal_depth * offset_x * inverse
    slope_y = focal_depth * offset_y * inverse
    first_row = [
        (focal_depth * rotation[0][index] - slope_x * rotation[2][index]) * scales[index]
        for index in range(3)
    ]
    second_row = [
        (focal_depth * rotation[1][index] - slope_y * rotation[2][index]) * scales[index]
        for index in range(3)
    ]
    sigma_xx = (
        first_row[0] * first_row[0]
        + first_row[1] * first_row[1]
        + first_row[2] * first_row[2]
        + BLUR
    )
    sigma_xy = (
        first_row[0] * second_row[0] + first_row[1] * second_row[1] + first_row[2] * second_row[2]
    )
    sigma_yy = (
        second_row[0] * second_row[0]
        + second_row[1] * second_row[1]
        + second_row[2] * second_row[2]
        + BLUR
    )
    determinant = sigma_xx * sigma_yy - sigma_xy * sigma_xy
    distance = jnp.sqrt(offset_x * offset_x + offset_y * offset_y + depth * depth)
    basis = sh_basis(offset_x / distance, offset_y / distance, depth / distance)
    colors = []
    for channel in range(3):
        total = basis[0] * rows[11 + channel]
        for index in range(1, 16):
            total = total + basis[index] * rows[11 + 3 * index + channel]
        colors.append(jnp.maximum(total + 0.5, 0.0))
    return [
        screen_x,
        screen_y,
        sigma_yy / determinant,
        -sigma_xy / determinant,
        sigma_xx / determinant,
        colors[0],
        colors[1],
        colors[2],
    ]


def code_rows(params_ref, blocks_here):
    rows = []
    for row in range(PARAMS):
        parts = [
            params_ref[row : row + 1, block * BLOCK : (block + 1) * BLOCK]
            for block in range(blocks_here)
        ]
        rows.append(jnp.concatenate(parts + parts, axis=0))
    return rows


def code_shift(blocks_here):
    code = lax.broadcasted_iota(jnp.int32, (2 * blocks_here, BLOCK), 0)
    return jnp.where(code >= blocks_here, BASELINE, 0.0).astype(jnp.float32)


def halves(values, pieces):
    out = []
    rest = values
    for index in range(pieces):
        part = rest.astype(jnp.bfloat16)
        out.append(part)
        if index < pieces - 1:
            rest = rest - part.astype(jnp.float32)
    return out


def project_kernel(
    blocks_here,
    center_x,
    center_y,
    codes_hbm,
    params_hbm,
    out_hbm,
    codes_ref,
    params_ref,
    table_ref,
    out_ref,
    sems,
    out_sems,
):
    copies = [pltpu.make_async_copy(codes_hbm, codes_ref, sems.at[blocks_here])]
    for block in range(blocks_here):
        where = (slice(None), pl.ds(block * BLOCK, BLOCK))
        copies.append(
            pltpu.make_async_copy(params_hbm.at[where], params_ref.at[where], sems.at[block])
        )
    for copy in copies:
        copy.start()
    for copy in copies[1:]:
        copy.wait()
    rows = code_rows(params_ref, blocks_here)
    shown = project(rows, code_shift(blocks_here), center_x, center_y)
    shown = shown[:5] + [jax.nn.sigmoid(rows[10])] + shown[5:]
    for code in range(2 * blocks_here):
        for feat in range(FEATS):
            table_ref[code, feat : feat + 1] = shown[feat][code : code + 1]
    copies[0].wait()

    def fill(target, carry):
        code = jnp.maximum(codes_ref[target], 0)
        out_ref[pl.ds(target * FEATS, 8)] = table_ref[code, 0:8]
        out_ref[pl.ds(target * FEATS + 8, 1)] = table_ref[code, 8:9]
        return carry

    rows = out_ref.shape[0] // OUT_PARTS
    parts = []
    for index in range(OUT_PARTS):
        first = index * (rows // FEATS)
        lax.fori_loop(first, first + rows // FEATS, fill, 0, unroll=32)
        where = pl.ds(index * rows, rows)
        parts.append(
            pltpu.make_async_copy(out_ref.at[where], out_hbm.at[where], out_sems.at[index])
        )
        parts[-1].start()
    for part in parts:
        part.wait()


def render_kernel(
    tiles_y,
    scalars_ref,
    slots_ref,
    goal_ref,
    out_ref,
    alpha_ref,
    weight_ref,
    pieces_ref,
    carry_ref,
    color_ref,
    slope_ref,
):
    tiles = goal_ref.shape[0]
    per_view = TILES_X * tiles_y
    f32 = jnp.float32
    half = SIDE // 2
    lane = lax.broadcasted_iota(jnp.int32, (2 * BLOCK, 2 * BLOCK), 1)
    depth = lax.broadcasted_iota(jnp.int32, (2 * BLOCK, 2 * BLOCK), 0) % BLOCK
    earlier = jnp.where((lane >= BLOCK) | (depth < lane), 1.0, 0.0).astype(jnp.bfloat16)
    later = jnp.where((lane >= BLOCK) | (depth > lane), 1.0, 0.0).astype(jnp.bfloat16)
    ones = jnp.ones((2 * BLOCK, BLOCK), jnp.bfloat16)
    column = lax.broadcasted_iota(jnp.int32, (half, BLOCK), 0).astype(f32) - (SIDE / 2 - 0.5)

    out_ref[...] = jnp.zeros_like(out_ref)

    def entry_of(tile, layer):
        return scalars_ref[tiles + tile * LIST + layer]

    def feature(slot, index):
        return slots_ref[pl.ds(slot * FEATS + index, 1)]

    def wide(row):
        return jnp.broadcast_to(row, (half, BLOCK))

    def center(tile):
        within = lax.rem(scalars_ref[tile], per_view)
        middle_x = (lax.rem(within, TILES_X) * SIDE + half).astype(f32)
        middle_y = (lax.div(within, TILES_X) * SIDE + half).astype(f32)
        return middle_x, middle_y

    def row_of(index, part):
        start = index * SIDE + part * half
        return slice(start, start + half)

    def offsets(tile, slot):
        middle_x, middle_y = center(tile)
        place_x = wide(feature(slot, 0) - middle_x)
        place_y = wide(feature(slot, 1) - middle_y)
        return [column + part * half - place_x for part in range(2)], place_y

    def split_row(tile, row, parts):
        pairs = [halves(part, 2) for part in parts]
        start = tile * TILE + row * SIDE
        for side in range(2):
            both = jnp.concatenate([pair[side] for pair in pairs], axis=0)
            pieces_ref[start : start + SIDE, side * BLOCK : (side + 1) * BLOCK] = both

    def add_up(matrix):
        return jnp.concatenate(
            [
                jnp.dot(
                    pieces_ref[tile * TILE : (tile + 1) * TILE],
                    matrix,
                    preferred_element_type=f32,
                )
                for tile in range(tiles)
            ],
            axis=0,
        )

    def forward(layer, carry):
        for tile in range(tiles):
            entry = entry_of(tile, layer)
            slot = jnp.maximum(entry, 0)
            live = jnp.where(entry >= 0, 1.0, 0.0).astype(f32)
            delta_x, place_y = offsets(tile, slot)
            scale = jnp.float32(LOG2_E)
            brightness = wide(jnp.log(feature(slot, 5) * live) * scale)
            half_x = [
                wide((-0.5 * scale) * feature(slot, 2)) * delta * delta + brightness
                for delta in delta_x
            ]
            cross = [wide(-scale * feature(slot, 3)) * delta for delta in delta_x]
            half_y = wide((-0.5 * scale) * feature(slot, 4))
            for row in range(SIDE):
                delta_y = (row - (SIDE / 2 - 0.5)) - place_y
                scaled_y = half_y * delta_y
                logs = []
                for part in range(2):
                    power = half_x[part] + delta_y * (cross[part] + scaled_y)
                    alpha = jnp.exp2(power)
                    alpha_ref[tile, layer, row_of(row, part)] = alpha
                    logs.append(jnp.log(1.0 - alpha))
                split_row(tile, row, logs)
        sums = add_up(earlier)
        for tile in range(tiles):
            slot = jnp.maximum(entry_of(tile, layer), 0)
            shades = [wide(feature(slot, 6 + channel)) for channel in range(3)]
            for row in range(SIDE):
                for part in range(2):
                    where = row_of(row, part)
                    start = tile * TILE + where.start
                    before = carry_ref[tile, where]
                    weight = alpha_ref[tile, layer, where] * jnp.exp(
                        sums[start : start + half, :BLOCK] + before
                    )
                    weight_ref[tile, layer, where] = weight
                    carry_ref[tile, where] = before + sums[start : start + half, BLOCK:]
                    for channel in range(3):
                        color_ref[tile, channel, where] += weight * shades[channel]
        return carry

    color_ref[...] = jnp.zeros_like(color_ref)
    carry_ref[...] = jnp.zeros_like(carry_ref)
    lax.fori_loop(0, LIST, forward, 0, unroll=8)

    for tile in range(tiles):
        goals = jnp.concatenate([goal_ref[tile], jnp.zeros((5, TILE), f32)], axis=0).T
        for channel in range(3):
            high, low = halves(color_ref[tile, channel], 2)
            color = jnp.dot(
                jnp.concatenate([high, low], axis=1), ones, preferred_element_type=f32
            )
            error = color - goals[:, channel : channel + 1]
            slope_ref[tile, channel] = error * lax.rsqrt(error * error + SMOOTHING) * (1.0 / 3.0)
    carry_ref[...] = jnp.zeros_like(carry_ref)

    def total(values):
        return jnp.sum(values, axis=0, keepdims=True)

    def backward(step, carry):
        layer = LIST - 1 - step
        color_grads = []
        for tile in range(tiles):
            slot = jnp.maximum(entry_of(tile, layer), 0)
            shades = [wide(feature(slot, 6 + channel)) for channel in range(3)]
            grads = [jnp.zeros((half, BLOCK), f32) for _ in range(3)]
            for row in range(SIDE):
                parts = []
                for part in range(2):
                    where = row_of(row, part)
                    weight = weight_ref[tile, layer, where]
                    pulled = [weight * slope_ref[tile, channel, where] for channel in range(3)]
                    grads = [grads[channel] + pulled[channel] for channel in range(3)]
                    gain = pulled[0] * shades[0] + pulled[1] * shades[1] + pulled[2] * shades[2]
                    weight_ref[tile, layer, where] = gain
                    parts.append(gain)
                split_row(tile, row, parts)
            color_grads.append([total(grad) for grad in grads])
        sums = add_up(later)
        for tile in range(tiles):
            slot = jnp.maximum(entry_of(tile, layer), 0)
            delta_x, place_y = offsets(tile, slot)
            flat = [jnp.zeros((half, BLOCK), f32) for _ in range(2)]
            tilt = [jnp.zeros((half, BLOCK), f32) for _ in range(2)]
            bend = jnp.zeros((half, BLOCK), f32)
            for row in range(SIDE):
                delta_y = (row - (SIDE / 2 - 0.5)) - place_y
                for part in range(2):
                    where = row_of(row, part)
                    start = tile * TILE + where.start
                    alpha = alpha_ref[tile, layer, where]
                    after = carry_ref[tile, where]
                    behind = sums[start : start + half, :BLOCK] + after
                    carry_ref[tile, where] = after + sums[start : start + half, BLOCK:]
                    power_grad = weight_ref[tile, layer, where] - behind * (alpha / (1.0 - alpha))
                    turned = power_grad * delta_y
                    flat[part] += power_grad
                    tilt[part] += turned
                    bend += turned * delta_y
            leaned = [flat[part] * delta_x[part] for part in range(2)]
            sum_x = total(leaned[0] + leaned[1])
            sum_y = total(tilt[0] + tilt[1])
            conic_a, conic_b, conic_c = feature(slot, 2), feature(slot, 3), feature(slot, 4)
            results = [
                conic_a * sum_x + conic_b * sum_y,
                conic_b * sum_x + conic_c * sum_y,
                -0.5 * total(leaned[0] * delta_x[0] + leaned[1] * delta_x[1]),
                -total(tilt[0] * delta_x[0] + tilt[1] * delta_x[1]),
                -0.5 * total(bend),
                total(flat[0] + flat[1]),
            ] + color_grads[tile]
            for index in range(FEATS):
                out_ref[pl.ds(slot * FEATS + index, 1)] += results[index]
        return carry

    lax.fori_loop(0, LIST, backward, 0, unroll=8)


def collect_kernel(keys_ref, slots_ref, out_ref):
    copies, count = out_ref.shape[:2]
    width = slots_ref.shape[0]
    wanted = lax.broadcasted_iota(jnp.int32, (count, width), 0)
    picker = jnp.where(keys_ref[...] == wanted, 1.0, 0.0).astype(jnp.bfloat16)
    total = jnp.zeros((count, BLOCK), jnp.float32)
    for piece in halves(slots_ref[...], 3):
        total += jnp.dot(picker, piece, preferred_element_type=jnp.float32)
    for copy in range(copies):
        out_ref[copy] = total


def update_kernel(
    blocks_here,
    center_x,
    center_y,
    cot_ref,
    params_ref,
    adam_m_ref,
    adam_v_ref,
    new_params_ref,
    new_m_ref,
    new_v_ref,
    grad_ref,
):
    codes = 2 * blocks_here
    rows = code_rows(params_ref, blocks_here)
    shift = code_shift(blocks_here)
    summed = cot_ref[0]
    for group in range(1, cot_ref.shape[0]):
        summed = summed + cot_ref[group]
    cots = [summed[codes * feat : codes * (feat + 1)] for feat in range(FEATS)]
    used = rows[:10] + rows[11:]

    def shown_of(values):
        return project(values[:10] + [None] + values[10:], shift, center_x, center_y)

    _, pull = jax.vjp(shown_of, used)
    grads = pull(cots[:5] + cots[6:])[0]
    logit_grad = cots[5] * (1.0 - jax.nn.sigmoid(rows[10]))
    grads = grads[:10] + [logit_grad] + grads[10:]
    for row in range(PARAMS):
        both = grads[row][:blocks_here] + grads[row][blocks_here:]
        for block in range(blocks_here):
            grad_ref[row : row + 1, block * BLOCK : (block + 1) * BLOCK] = both[block : block + 1]
    grad = grad_ref[...]
    new_m = BETA_ONE * adam_m_ref[...] + (1.0 - BETA_ONE) * grad
    new_v = BETA_TWO * adam_v_ref[...] + (1.0 - BETA_TWO) * grad * grad
    m_hat = new_m * (1.0 / (1.0 - BETA_ONE**ADAM_STEP))
    v_hat = new_v * (1.0 / (1.0 - BETA_TWO**ADAM_STEP))
    row = lax.broadcasted_iota(jnp.int32, grad.shape, 0)
    rates = jnp.full(grad.shape, RATES[0][1], jnp.float32)
    for first, rate in RATES[1:]:
        rates = jnp.where(row >= first, jnp.float32(rate), rates)
    new_params_ref[...] = params_ref[...] - rates * m_hat / (jnp.sqrt(v_hat) + ADAM_EPS)
    new_m_ref[...] = new_m
    new_v_ref[...] = new_v


def vmem(count):
    return [pl.BlockSpec(memory_space=VMEM)] * count


def smem(count):
    return [pl.BlockSpec(memory_space=SMEM)] * count


def run_project(params, provided, center_x, center_y, limit):
    blocks_here = params.shape[1] // BLOCK
    codes = 2 * blocks_here
    f32 = jnp.float32
    return pl.pallas_call(
        lambda *refs: project_kernel(blocks_here, center_x, center_y, *refs),
        out_shape=jax.ShapeDtypeStruct((provided.shape[0] * FEATS, BLOCK), f32),
        in_specs=[pl.BlockSpec(memory_space=pltpu.MemorySpace.HBM)] * 2,
        out_specs=pl.BlockSpec(memory_space=pl.ANY),
        scratch_shapes=[
            pltpu.SMEM(provided.shape, jnp.int32),
            pltpu.VMEM(params.shape, f32),
            pltpu.VMEM((codes, FEATS, BLOCK), f32),
            pltpu.VMEM((provided.shape[0] * FEATS, BLOCK), f32),
            pltpu.SemaphoreType.DMA((blocks_here + 1,)),
            pltpu.SemaphoreType.DMA((OUT_PARTS,)),
        ],
        compiler_params=pltpu.CompilerParams(vmem_limit_bytes=WHOLE_VMEM),
        name="project",
    )(provided, params)


def run_render(scalars, incoming, goals, tiles_y, limit):
    tiles = goals.shape[0]
    f32 = jnp.float32
    pairs = pltpu.VMEM((tiles, LIST, TILE, BLOCK), f32)
    return pl.pallas_call(
        lambda *refs: render_kernel(tiles_y, *refs),
        out_shape=jax.ShapeDtypeStruct(incoming.shape, f32),
        in_specs=smem(1) + vmem(2),
        out_specs=vmem(1)[0],
        scratch_shapes=[
            pairs,
            pairs,
            pltpu.VMEM((tiles * TILE, 2 * BLOCK), jnp.bfloat16),
            pltpu.VMEM((tiles, TILE, BLOCK), f32),
            pltpu.VMEM((tiles, 3, TILE, BLOCK), f32),
            pltpu.VMEM((tiles, 3, TILE, BLOCK), f32),
        ],
        compiler_params=limit,
        name="render",
    )(scalars, incoming, goals)


def run_collect(keys, returned, codes, groups, limit):
    return pl.pallas_call(
        collect_kernel,
        out_shape=jax.ShapeDtypeStruct((groups, FEATS * codes, BLOCK), jnp.float32),
        in_specs=vmem(2),
        out_specs=vmem(1)[0],
        compiler_params=limit,
        name="collect",
    )(keys, returned)


def run_update(gathered, params, adam_m, adam_v, center_x, center_y, limit):
    blocks_here = params.shape[1] // BLOCK
    shape = jax.ShapeDtypeStruct(params.shape, jnp.float32)
    return pl.pallas_call(
        lambda *refs: update_kernel(blocks_here, center_x, center_y, *refs),
        out_shape=(shape,) * 4,
        in_specs=vmem(4),
        out_specs=tuple(vmem(4)),
        compiler_params=limit,
        name="update",
    )(gathered, params, adam_m, adam_v)


def exchange(slots, dev_count):
    sent = slots.reshape(dev_count, 1, SLOT)
    return lax.all_to_all(sent, "dev", split_axis=0, concat_axis=0, tiled=True).reshape(slots.shape)


def on_device(params, adam_m, adam_v, target, tile_ids, send_blocks, tile_lists):
    dev_count = lax.axis_size("dev")
    blocks_here = params.shape[1] // BLOCK
    codes = 2 * blocks_here
    tiles_y = dev_count * blocks_here // TILES_X
    center_x = 8.0 * TILES_X
    center_y = 8.0 * tiles_y
    limit = pltpu.CompilerParams(vmem_limit_bytes=VMEM_LIMIT)
    provided = send_blocks.reshape(-1)
    scalars = jnp.concatenate([tile_ids.reshape(-1), tile_lists.reshape(-1)])
    order = jnp.arange(FEATS, dtype=jnp.int32) * codes
    keys = jnp.where(provided[:, None] >= 0, provided[:, None] + order[None, :], -1)
    keys = keys.reshape(1, dev_count * FEATS)
    scalars, keys = lax.optimization_barrier((scalars, keys))

    outgoing = run_project(params, provided, center_x, center_y, limit)
    incoming = exchange(outgoing, dev_count)
    goals = target.reshape(target.shape[2:])
    cotangent = run_render(scalars, incoming, goals, tiles_y, limit)
    returned = exchange(cotangent, dev_count)
    groups = lax.axis_size("rep")
    per_code = run_collect(keys, returned, codes, groups, limit)
    gathered = lax.all_to_all(per_code, "rep", split_axis=0, concat_axis=0, tiled=True)
    return run_update(gathered, params, adam_m, adam_v, center_x, center_y, limit)


def solution(mesh):
    placed = (
        P(None, "dev"),
        P(None, "dev"),
        P(None, "dev"),
        P("rep", "dev", None, None, None),
        P("rep", "dev", None),
        P("rep", "dev", None, None),
        P("rep", "dev", None, None),
    )
    return jax.shard_map(
        on_device,
        mesh=mesh,
        in_specs=placed,
        out_specs=(P(None, "dev"), P(None, "dev"), P(None, "dev"), P(None, "dev")),
        check_vma=False,
    )
```
